32 devices in a mesh: groups: 2 (over x), frame: 16 (over z, y, core).
Axes of the slice: x: 2, y: 2, z: 4, core: 2. Of those that a mesh axis runs over, the one named last changes fastest.
Arguments:
- frames_in: bfloat16 [32, 256, 2240], P(('groups', 'frame')), parts along dimension 0, may hold values from -16 to 16
- qkv_weight: bfloat16 [3, 2240, 1280], P(None, None, 'frame'), may hold values from -0.125 to 0.125
Outputs:
- attended: bfloat16 [32, 256, 1280], P(('groups', 'frame')), parts along dimension 0
The draws below stay inside these ranges and needn't reach their ends.
There are 2 independent parts, one for each index of `groups`. The reference program is written for one: setup_inputs(seed, part) draws one part's arguments, and reference() takes and returns one part's arrays. A program takes and returns all parts, laid end to end along the dimension named above; an argument that names none is the same for every part. Nothing has to cross between parts.
All inputs are finite; a program needn't handle non-finite values.
Results may differ from the reference program's by a relative error of at most 0.0039.
Values may be sent and summed in bfloat16 or wider, within the bound.
No kernel may reach another device: no remote copies, remote signals or barrier semaphores. Data moves between devices by JAX's collectives and lax.ppermute only.
A program may use at most 128 MiB of HBM per device.

```python
import math
import jax
import jax.numpy as jnp
from jax import lax

D = 2240
HEAD_DIM = 32
HEADS = 40
FH = 8
FW = 32
HD = 1280
FRAMES = 16


def draw_frames_in(key, part):
    key_shared, key_frame, key_token = jax.random.split(jax.random.fold_in(key, 11), 3)
    shared = jax.random.normal(key_shared, (1, 1, D), jnp.float32) * 0.7
    frame_part = jax.random.normal(key_frame, (FRAMES, 1, D), jnp.float32) * 0.7
    token_part = jax.random.normal(key_token, (FRAMES, FH * FW, D), jnp.float32)
    position = jnp.arange(FRAMES, dtype=jnp.float32) / max(FRAMES - 1, 1)
    rising = jnp.exp(position * math.log(3.0))[:, None, None]
    values = jnp.clip(rising * (shared + frame_part + token_part), -16.0, 16.0)
    return values.astype(jnp.bfloat16)


def levels(own_key, dims, cuts, low, largest):
    factor_of = 1.0
    for axis_at, blocks in cuts:
        steps = jax.random.uniform(jax.random.fold_in(jax.random.fold_in(own_key, 6), axis_at), (blocks,), jnp.float32, low / len(cuts), largest / len(cuts))
        factor_of = factor_of * jnp.repeat(jnp.exp(steps), dims[axis_at] // blocks).reshape((-1,) + (1,) * (len(dims) - 1 - axis_at))
    return factor_of


def noise(rng, extent, deviation, bound, shards=(), kind=jnp.bfloat16):
    values = deviation * jax.random.normal(rng, extent, jnp.float32)
    if shards:
        values = values * levels(rng, extent, shards, -0.22, 0.18)
    return jnp.clip(values, -bound, bound).astype(kind)


def setup_inputs(seed: int = 0, part: int = 0) -> dict:
    seeds = jax.random.split(jax.random.key(seed), 3)
    part_splits = jax.random.split(jax.random.fold_in(seeds[2], part), 3)
    return {
        "frames_in": draw_frames_in(jax.random.fold_in(jax.random.fold_in(seeds[2], part), 71), part),
        "qkv_weight": noise(seeds[1], (3, D, HD), D ** -0.5, 0.125, ((2, 16),)),
    }


EPSILON = 1e-6


def reference(frames_in, qkv_weight):
    def frame_step(carry, frame):
        prior_state, prior_keys = carry
        queries = jnp.dot(frame, qkv_weight[0], preferred_element_type=jnp.float32)
        key_rows = jnp.dot(frame, qkv_weight[1], preferred_element_type=jnp.float32).astype(jnp.bfloat16)
        value_rows = jnp.dot(frame, qkv_weight[2], preferred_element_type=jnp.float32).astype(jnp.bfloat16)
        feature_k = jax.nn.relu(key_rows).astype(jnp.float32).reshape(-1, HEADS, HEAD_DIM)
        values = value_rows.astype(jnp.float32).reshape(-1, HEADS, HEAD_DIM)
        local_state = jnp.einsum("thi,thj->hij", feature_k, values, precision=lax.Precision.HIGHEST)
        local_keys = jnp.sum(feature_k, axis=0)
        total_state = prior_state + local_state
        total_keys = prior_keys + local_keys
        feature_q = jax.nn.relu(queries).reshape(-1, HEADS, HEAD_DIM)
        numer = jnp.einsum("thi,hij->thj", feature_q, total_state, precision=lax.Precision.HIGHEST)
        denom = jnp.einsum("thi,hi->th", feature_q, total_keys, precision=lax.Precision.HIGHEST)
        result = (numer / (denom[:, :, None] + EPSILON)).astype(jnp.bfloat16)
        return (total_state, total_keys), result.reshape(-1, HEADS * HEAD_DIM)

    start_state = jnp.zeros((HEADS, HEAD_DIM, HEAD_DIM), jnp.float32)
    start_keys = jnp.zeros((HEADS, HEAD_DIM), jnp.float32)
    final_carry, outputs = lax.scan(frame_step, (start_state, start_keys), frames_in)
    return outputs
```

```python
import jax
import jax.numpy as jnp
from jax import lax
from jax.sharding import PartitionSpec as P

HEAD_DIM = 32
EPSILON = 1e-06
AXES = ("groups", "frame")


def dot(a, b, dims):
    return lax.dot_general(a, b, (dims, ((), ())), preferred_element_type=jnp.float32)


def gathered_plan(frames_in, qkv_weight):
    tokens = frames_in[0]
    count = tokens.shape[0]
    weights = lax.all_gather(qkv_weight, "frame", axis=2, tiled=True)
    projected = jnp.einsum("td,sdc->stc", tokens, weights, preferred_element_type=jnp.float32)
    heads = weights.shape[2] // HEAD_DIM
    split = lambda a: a.reshape(count, heads, HEAD_DIM)
    queries = split(jax.nn.relu(projected[0]))
    keys = split(jax.nn.relu(projected[1].astype(jnp.bfloat16)))
    values = split(projected[2].astype(jnp.bfloat16))
    state = jnp.einsum("thi,thj->hij", keys, values, preferred_element_type=jnp.float32)
    key_sum = jnp.sum(keys.astype(jnp.float32), axis=0)
    both = jnp.concatenate([state, key_sum[:, :, None]], axis=2)
    everyone = lax.all_gather(both.reshape(heads, -1), "frame")
    upto = jnp.arange(everyone.shape[0]) <= lax.axis_index("frame")
    total = jnp.sum(jnp.where(upto[:, None, None], everyone, 0.0), axis=0).reshape(both.shape)
    result = jnp.einsum("thi,hij->thj", queries, total, precision=lax.Precision.HIGHEST)
    attended = result[..., :HEAD_DIM] / (result[..., HEAD_DIM:] + EPSILON)
    return attended.astype(jnp.bfloat16).reshape(1, count, -1)


class Layout:
    def __init__(self, mesh):
        self.frames = mesh.shape["frame"]
        self.lows = 2
        self.highs = self.frames // 4

    def pairs(self, target, source=lambda g, hi, b, lo: True):
        out = []
        for g in range(2):
            for hi in range(self.highs):
                for b in range(2):
                    for lo in range(self.lows):
                        if source(g, hi, b, lo):
                            to = target(g, hi, b, lo)
                            out.append((self.place(g, hi, b, lo), self.place(*to)))
        return out

    def place(self, g, hi, b, lo):
        return ((g * self.highs + hi) * 2 + b) * self.lows + lo


def send(a, pairs):
    return lax.ppermute(a, AXES, pairs)


def shared_plan(layout, frames_in, qkv_weight):
    g = lax.axis_index("groups")
    place = lax.axis_index("frame")
    lo, b, hi = place % 2, (place // 2) % 2, place // 4
    weights = qkv_weight.transpose(0, 2, 1)
    width, depth = weights.shape[1:]
    half = HEAD_DIM // 2
    own = frames_in[0].T
    count = own.shape[1]

    keeper = lambda g, hi, b, lo: lo == g
    other = lambda g, hi, b, lo: lo != g
    along = lambda k: lambda g, hi, b, lo: (g, hi ^ k, b, lo)
    over_b = layout.pairs(lambda g, hi, b, lo: (g, hi, 1 - b, lo))
    over_g = layout.pairs(lambda g, hi, b, lo: (1 - g, hi, b, lo))
    over_gb = layout.pairs(lambda g, hi, b, lo: (1 - g, hi, 1 - b, lo))
    swap = lambda g, hi, b, lo: (g, hi, b, 1 - lo)
    over_lo = layout.pairs(swap)

    extra = lax.dynamic_slice_in_dim(weights[:2], g * (width - half), half, axis=1)
    mains, extras = [weights], [extra]
    for got, kind in ((mains, keeper), (extras, other)):
        far = send(got[0], layout.pairs(along(2), kind))
        near = send(got[0], layout.pairs(along(1), kind))
        got.extend([near, far, send(far, layout.pairs(along(1), kind))])
    mine = lo == g
    mains = [jnp.where(mine, a, send(a, layout.pairs(swap, keeper))) for a in mains]
    extras = [jnp.where(mine, send(a, layout.pairs(swap, other)), a) for a in extras]

    next_b = send(own, over_b)
    next_g = send(own, over_g)
    cut = depth // 2
    across = jnp.concatenate([send(next_b[:cut], over_g), send(next_g[cut:], over_b)], axis=0)
    tokens = [own, next_b, next_g, across]

    rows = jnp.arange(width + half)
    key_head = (4 * half * g + (rows + half * g) % (width + half)) // HEAD_DIM
    value_head = (width * g + jnp.arange(width)) // HEAD_DIM
    same = value_head[:, None] == key_head[None, :]

    def project(k, m):
        main = dot(mains[k].reshape(3 * width, depth), tokens[m], ((1,), (0,)))
        more = dot(extras[k].reshape(2 * half, depth), tokens[m], ((1,), (0,)))
        queries = jnp.concatenate([main[:width], more[:half]], axis=0)
        keys = jnp.concatenate([main[width : 2 * width], more[half:]], axis=0)
        return (
            jax.nn.relu(queries).astype(jnp.bfloat16),
            jax.nn.relu(keys).astype(jnp.bfloat16),
            main[2 * width :].astype(jnp.bfloat16),
        )

    queries = [[None] * 4 for _ in range(4)]
    states, key_sums = [], []
    for m in range(4):
        frame_states, frame_keys = [], []
        for k in range(4):
            queries[m][k], keys, values = project(k, m)
            full = dot(values, keys, ((1,), (1,)))
            full = jnp.where(same, full, 0.0)
            frame_states.append(full[:, :32] + full[:, 32:64] + full[:, 64:])
            frame_keys.append(jnp.sum(keys.astype(jnp.float32), axis=1))
        states.append(jnp.concatenate(frame_states, axis=1))
        key_sums.append(jnp.concatenate([jnp.pad(jnp.stack(frame_keys), ((0, 4), (0, 32)))], axis=1))
    mine_all = jnp.stack([jnp.concatenate([s, t], axis=0) for s, t in zip(states, key_sums)])
    other_all = send(mine_all, over_lo)
    both = mine_all + other_all
    plane = jnp.stack([both[0] + both[1], both[2] + both[3]])
    before = jnp.zeros_like(plane)
    for k in (1, 2, 3):
        got = send(plane, layout.pairs(along(k)))
        lanes = [got[:, :width, 32 * (j ^ k) : 32 * (j ^ k) + 32] for j in range(4)]
        sums = [got[:, width + (j ^ k)][:, None] for j in range(4)] + [got[:, width + 4 :]]
        got = jnp.concatenate([jnp.concatenate(lanes, axis=2)] + sums, axis=1)
        before = before + jnp.where((hi ^ k) < hi, got, 0.0)

    outs = []
    for m in range(4):
        this_b = b ^ (m & 1)
        upto = before[m // 2] + mine_all[m]
        upto = upto + jnp.where(lo == 1, other_all[m], 0.0) + jnp.where(this_b == 1, both[m ^ 1], 0.0)
        blocks = []
        for k in range(4):
            part = upto[:width, 32 * k : 32 * k + 32]
            state = jnp.where(same, jnp.concatenate([part] * 3, axis=1), 0.0)
            key_sum = jnp.where(same, upto[width + k, : width + half][None, :], 0.0)
            q = queries[m][k]
            numer = dot(state.astype(jnp.bfloat16), q, ((1,), (0,)))
            denom = dot(key_sum.astype(jnp.bfloat16), q, ((1,), (0,)))
            blocks.append((numer / (denom + EPSILON)).astype(jnp.bfloat16))
        outs.append(jnp.stack(blocks))
    got = [outs[0], send(outs[1], over_b), send(outs[2], over_g), send(outs[3], over_gb)]

    every = jnp.stack(got).reshape(2, 2, 2, 2, width, count)
    for axis, bit in ((0, g), (1, b), (2, hi // 2), (3, hi % 2)):
        every = jnp.where(bit == 1, jnp.flip(every, axis), every)
    return every.transpose(5, 2, 3, 1, 0, 4).reshape(1, count, -1)


def solution(mesh):
    placed = (P(AXES, None, None), P(None, None, "frame"))

    def shards(frames_in, qkv_weight):
        width = qkv_weight.shape[2]
        if mesh.shape["groups"] == 2 and mesh.shape["frame"] == 16 and width * 2 == 5 * HEAD_DIM:
            return shared_plan(Layout(mesh), frames_in, qkv_weight)
        return gathered_plan(frames_in, qkv_weight)

    return jax.shard_map(
        shards, mesh=mesh, in_specs=placed, out_specs=P(AXES, None, None), check_vma=False
    )
```

```python
import jax
import jax.numpy as jnp
from jax import lax
from jax.experimental import pallas as pl
from jax.experimental.pallas import tpu as pltpu
from jax.sharding import PartitionSpec as P

HEAD_DIM = 32
EPSILON = 1e-06
AXES = ("groups", "frame")


def dot(a, b, dims):
    return lax.dot_general(a, b, (dims, ((), ())), preferred_element_type=jnp.float32)


def gathered_plan(frames_in, qkv_weight):
    tokens = frames_in[0]
    count = tokens.shape[0]
    weights = lax.all_gather(qkv_weight, "frame", axis=2, tiled=True)
    projected = jnp.einsum("td,sdc->stc", tokens, weights, preferred_element_type=jnp.float32)
    heads = weights.shape[2] // HEAD_DIM
    split = lambda a: a.reshape(count, heads, HEAD_DIM)
    queries = split(jax.nn.relu(projected[0]))
    keys = split(jax.nn.relu(projected[1].astype(jnp.bfloat16)))
    values = split(projected[2].astype(jnp.bfloat16))
    state = jnp.einsum("thi,thj->hij", keys, values, preferred_element_type=jnp.float32)
    key_sum = jnp.sum(keys.astype(jnp.float32), axis=0)
    both = jnp.concatenate([state, key_sum[:, :, None]], axis=2)
    everyone = lax.all_gather(both.reshape(heads, -1), "frame")
    upto = jnp.arange(everyone.shape[0]) <= lax.axis_index("frame")
    total = jnp.sum(jnp.where(upto[:, None, None], everyone, 0.0), axis=0).reshape(both.shape)
    result = jnp.einsum("thi,hij->thj", queries, total, precision=lax.Precision.HIGHEST)
    attended = result[..., :HEAD_DIM] / (result[..., HEAD_DIM:] + EPSILON)
    return attended.astype(jnp.bfloat16).reshape(1, count, -1)


class Layout:
    def __init__(self, mesh):
        self.frames = mesh.shape["frame"]
        self.lows = 2
        self.highs = self.frames // 4

    def pairs(self, target, source=lambda g, hi, b, lo: True):
        out = []
        for g in range(2):
            for hi in range(self.highs):
                for b in range(2):
                    for lo in range(self.lows):
                        if source(g, hi, b, lo):
                            to = target(g, hi, b, lo)
                            out.append((self.place(g, hi, b, lo), self.place(*to)))
        return out

    def place(self, g, hi, b, lo):
        return ((g * self.highs + hi) * 2 + b) * self.lows + lo


def send(a, pairs):
    return lax.ppermute(a, AXES, pairs)


ANY = pl.BlockSpec(memory_space=pl.ANY)
VMEM = pl.BlockSpec(memory_space=pltpu.VMEM)
SMEM = pl.BlockSpec(memory_space=pltpu.SMEM)
LIGHT = pl.CostEstimate(flops=1000, bytes_accessed=1000, transcendentals=0)


def call(body, out, ins, scratch, *operands):
    return pl.pallas_call(
        body,
        out_shape=out,
        in_specs=ins,
        out_specs=jax.tree.map(lambda _: VMEM, out),
        scratch_shapes=scratch,
        compiler_params=pltpu.CompilerParams(vmem_limit_bytes=48 * 2**20),
        cost_estimate=LIGHT,
    )(*operands)


def heads_of(g, width, half):
    shape = (width, width + half)
    row = lax.broadcasted_iota(jnp.int32, shape, 0)
    column = lax.broadcasted_iota(jnp.int32, shape, 1)
    turned = column + half * g
    turned = jnp.where(turned >= width + half, turned - (width + half), turned)
    return (width * g + row) // HEAD_DIM == (4 * half * g + turned) // HEAD_DIM


def project(place, weights, frames, ks, carried=None):
    main_rows, depth = weights[0][0].shape
    extra_rows = weights[0][2].shape[0]
    width, half = main_rows // 3, extra_rows // 2
    count = frames[0][0].shape[1]
    nk, nm, parts = len(weights), len(frames), [len(f) for f in frames]
    carried = carried or []

    def body(place_ref, *refs):
        refs = list(refs)
        w_refs = [[refs.pop(0) for _ in range(4)] for _ in range(nk)]
        x_refs = [[refs.pop(0) for _ in range(n)] for n in parts]
        c_refs = [refs.pop(0) for _ in carried]
        q_ref, s_ref, w_all, x_all, w_sem, x_sem = refs
        g, lo = place_ref[0], place_ref[3]
        mine = lo == g

        def copies(k, own):
            main, extra = (w_refs[k][0], w_refs[k][3]) if own else (w_refs[k][1], w_refs[k][2])
            return (
                pltpu.make_async_copy(main, w_all.at[k, :main_rows], w_sem.at[k, 0]),
                pltpu.make_async_copy(extra, w_all.at[k, main_rows:], w_sem.at[k, 1]),
            )

        def frame(m):
            size = depth // parts[m]
            return [
                pltpu.make_async_copy(x, x_all.at[m, size * i : size * (i + 1)], x_sem.at[m, i])
                for i, x in enumerate(x_refs[m])
            ]

        def start_weights(k):
            @pl.when(mine)
            def _():
                for c in copies(k, True):
                    c.start()

            @pl.when(jnp.logical_not(mine))
            def _():
                for c in copies(k, False):
                    c.start()

        start_weights(0)
        for m in range(nm):
            for c in frame(m):
                c.start()
        for k in range(1, nk):
            start_weights(k)
        same = heads_of(g, width, half)
        s_ref[...] = jnp.zeros_like(s_ref)
        done = 0
        for c_ref in c_refs:
            s_ref[done : done + c_ref.shape[0]] = c_ref[...]
            done += c_ref.shape[0]
        ones = jnp.ones((8, count), jnp.bfloat16)
        for k in range(nk):
            for c in copies(k, True):
                c.wait()
            at = 32 * ks[k]

            def one(m, _):
                made = dot(w_all[k], x_all[m], ((1,), (0,)))
                q_ref[m, k, :width] = jnp.maximum(made[:width], 0.0)
                q_ref[m, k, width:] = jnp.maximum(made[3 * width : 3 * width + half], 0.0)
                keys = jnp.concatenate([made[width : 2 * width], made[3 * width + half :]], axis=0)
                keys = jnp.maximum(keys, 0.0).astype(jnp.bfloat16)
                values = made[2 * width : 3 * width].astype(jnp.bfloat16)
                full = jnp.where(same, dot(values, keys, ((1,), (1,))), 0.0)
                s_ref[m, :width, at : at + 32] = full[:, :32] + full[:, 32:64] + full[:, 64:]
                s_ref[m, width + ks[k] : width + ks[k] + 1, : width + half] = dot(ones, keys, ((1,), (1,)))[:1]
                return 0

            if k == 0:
                for m in range(nm):
                    for c in frame(m):
                        c.wait()
            lax.fori_loop(0, nm, one, 0)

    out = (
        jax.ShapeDtypeStruct((nm, nk, width + half, count), jnp.float32),
        jax.ShapeDtypeStruct((nm, width + 8, 128), jnp.float32),
    )
    scratch = [
        pltpu.VMEM((nk, main_rows + extra_rows, depth), jnp.bfloat16),
        pltpu.VMEM((nm, depth, count), jnp.bfloat16),
        pltpu.SemaphoreType.DMA((nk, 2)),
        pltpu.SemaphoreType.DMA((nm, 2)),
    ]
    flat = [a for w in weights for a in w] + [a for f in frames for a in f]
    ins = [SMEM] + [ANY] * len(flat) + [VMEM] * len(carried)
    return call(body, out, ins, scratch, place, *flat, *carried)


def plane_sum(mine, others):
    def body(a_ref, b_ref, out_ref):
        both = a_ref[...] + b_ref[...]
        out_ref[0] = both[0] + both[1]
        out_ref[1] = both[2] + both[3]

    out = jax.ShapeDtypeStruct((2,) + mine.shape[1:], jnp.float32)
    return call(body, out, [VMEM] * 2, [], mine, others)


def apply(place, ms, queries, mine, others, planes):
    arrays = []
    for row in queries:
        for a, _, _ in row:
            if not any(a is b for b in arrays):
                arrays.append(a)
    where = [[([a is b for b in arrays].index(True), m, k) for a, m, k in row] for row in queries]
    rows, count = arrays[0].shape[2:]
    width = mine.shape[1] - 8
    half = rows - width

    def body(place_ref, *refs):
        q_refs = refs[: len(arrays)]
        mine_ref, others_ref, *plane_refs = refs[len(arrays) : len(arrays) + 5]
        outs = refs[len(arrays) + 5 :]
        g, hi, b, lo = (place_ref[i] for i in range(4))
        same = heads_of(g, width, half)
        factor = lambda yes: jnp.where(yes, 1.0, 0.0).astype(jnp.float32)
        earlier = [factor(jnp.bitwise_xor(hi, k) < hi) for k in (1, 2, 3)]
        second = factor(lo == 1)

        def split(a):
            high = a.astype(jnp.bfloat16)
            return high, (a - high.astype(jnp.float32)).astype(jnp.bfloat16)

        for out_ref, m in zip(outs, ms):
            after = factor(jnp.bitwise_xor(b, m & 1) == 1)
            upto = mine_ref[m] + second * others_ref[m] + after * (mine_ref[m ^ 1] + others_ref[m ^ 1])
            for j in range(4):
                part = upto[:width, 32 * j : 32 * j + 32]
                sums = upto[width + j : width + j + 1, :rows]
                for k in (1, 2, 3):
                    i = j ^ k
                    part += earlier[k - 1] * plane_refs[k - 1][m // 2, :width, 32 * i : 32 * i + 32]
                    sums += earlier[k - 1] * plane_refs[k - 1][m // 2, width + i : width + i + 1, :rows]
                state = jnp.where(same, jnp.concatenate([part] * 3, axis=1), 0.0)
                sums = jnp.where(same, jnp.broadcast_to(sums, (width, rows)), 0.0)
                left, left_low = split(jnp.concatenate([state, sums], axis=0))
                a, qm, qk = where[m][j]
                q, q_low = split(q_refs[a][qm, qk])
                both = dot(left, q, ((1,), (0,))) + dot(left_low, q, ((1,), (0,))) + dot(left, q_low, ((1,), (0,)))
                out_ref[j] = (both[:width] / (both[width:] + EPSILON)).astype(jnp.bfloat16)

    out = [jax.ShapeDtypeStruct((4, width, count), jnp.bfloat16)] * len(ms)
    ins = [SMEM] + [VMEM] * (len(arrays) + 5)
    return call(body, out, ins, [], place, *arrays, mine, others, *planes)


def assemble(place, got):
    blocks, width, count = got[0].shape

    def body(place_ref, *refs):
        *got_refs, out_ref, every = refs
        g, hi, b = (place_ref[i] for i in range(3))
        for m in range(4):
            this_g, this_b = jnp.bitwise_xor(g, m >> 1), jnp.bitwise_xor(b, m & 1)
            for k in range(blocks):
                at = ((jnp.bitwise_xor(hi, k) * 2 + this_b) * 2 + this_g) * width
                every[pl.ds(pl.multiple_of(at, 16), width)] = got_refs[m][k]
        out_ref[...] = every[...].T

    out = jax.ShapeDtypeStruct((count, 4 * blocks * width), jnp.bfloat16)
    scratch = [pltpu.VMEM((4 * blocks * width, count), jnp.bfloat16)]
    return call(body, out, [SMEM] + [VMEM] * 4, scratch, place, *got)


def shared_plan(layout, frames_in, qkv_weight):
    g = lax.axis_index("groups")
    frame = lax.axis_index("frame")
    lo, b, hi = frame % 2, (frame // 2) % 2, frame // 4
    place = jnp.stack([g, hi, b, lo]).astype(jnp.int32)
    weights = qkv_weight.transpose(0, 2, 1)
    width, depth = weights.shape[1:]
    half = HEAD_DIM // 2
    own = frames_in[0].T

    keeper = lambda g, hi, b, lo: lo == g
    other = lambda g, hi, b, lo: lo != g
    along = lambda k: lambda g, hi, b, lo: (g, hi ^ k, b, lo)
    over_b = layout.pairs(lambda g, hi, b, lo: (g, hi, 1 - b, lo))
    over_g = layout.pairs(lambda g, hi, b, lo: (1 - g, hi, b, lo))
    over_gb = layout.pairs(lambda g, hi, b, lo: (1 - g, hi, 1 - b, lo))
    swap = lambda g, hi, b, lo: (g, hi, b, 1 - lo)
    over_lo = layout.pairs(swap)

    next_b = send(own, over_b)
    next_g = send(own, over_g)
    cut = depth // 2
    across = [send(next_b[:cut], over_g), send(next_g[cut:], over_b)]
    frames = [[own], [next_b], [next_g], across]

    extra = lax.dynamic_slice_in_dim(weights[:2], g * (width - half), half, axis=1)
    mains, extras = [weights.reshape(3 * width, depth)], [extra.reshape(2 * half, depth)]
    for got, kind in ((mains, keeper), (extras, other)):
        far = send(got[0], layout.pairs(along(2), kind))
        near = send(got[0], layout.pairs(along(1), kind))
        got.extend([near, far, send(far, layout.pairs(along(1), kind))])
    blocks = [
        (main, send(main, layout.pairs(swap, keeper)), extra, send(extra, layout.pairs(swap, other)))
        for main, extra in zip(mains, extras)
    ]

    q1, s1 = project(place, blocks[:3], frames[:3], [0, 1, 2])
    q2, s2 = project(place, blocks[:3], frames[3:], [0, 1, 2])
    q3, mine = project(place, blocks[3:], frames, [3], [s1, s2])
    queries = [[(q1, m, k) for k in range(3)] + [(q3, m, 0)] for m in range(3)]
    queries += [[(q2, 0, k) for k in range(3)] + [(q3, 3, 0)]]
    others = send(mine, over_lo)
    plane = plane_sum(mine, others)
    planes = [send(plane, layout.pairs(along(k))) for k in (1, 2, 3)]
    out1, out2, out3 = apply(place, [1, 2, 3], queries, mine, others, planes)
    (out0,) = apply(place, [0], queries, mine, others, planes)
    got = [out0, send(out1, over_b), send(out2, over_g), send(out3, over_gb)]
    return assemble(place, got)[None]


def solution(mesh):
    placed = (P(AXES, None, None), P(None, None, "frame"))

    def shards(frames_in, qkv_weight):
        width = qkv_weight.shape[2]
        if mesh.shape["groups"] == 2 and mesh.shape["frame"] == 16 and width * 2 == 5 * HEAD_DIM:
            return shared_plan(Layout(mesh), frames_in, qkv_weight)
        return gathered_plan(frames_in, qkv_weight)

    return jax.shard_map(
        shards, mesh=mesh, in_specs=placed, out_specs=P(AXES, None, None), check_vma=False
    )
```

```python
import jax
import jax.numpy as jnp
from jax import lax
from jax.experimental import pallas as pl
from jax.experimental.pallas import tpu as pltpu
from jax.sharding import PartitionSpec as P

HEAD_DIM = 32
EPSILON = 1e-06
AXES = ("groups", "frame")


def dot(a, b, dims):
    return lax.dot_general(a, b, (dims, ((), ())), preferred_element_type=jnp.float32)


def gathered_plan(frames_in, qkv_weight):
    tokens = frames_in[0]
    count = tokens.shape[0]
    weights = lax.all_gather(qkv_weight, "frame", axis=2, tiled=True)
    projected = jnp.einsum("td,sdc->stc", tokens, weights, preferred_element_type=jnp.float32)
    heads = weights.shape[2] // HEAD_DIM
    split = lambda a: a.reshape(count, heads, HEAD_DIM)
    queries = split(jax.nn.relu(projected[0]))
    keys = split(jax.nn.relu(projected[1].astype(jnp.bfloat16)))
    values = split(projected[2].astype(jnp.bfloat16))
    state = jnp.einsum("thi,thj->hij", keys, values, preferred_element_type=jnp.float32)
    key_sum = jnp.sum(keys.astype(jnp.float32), axis=0)
    both = jnp.concatenate([state, key_sum[:, :, None]], axis=2)
    everyone = lax.all_gather(both.reshape(heads, -1), "frame")
    upto = jnp.arange(everyone.shape[0]) <= lax.axis_index("frame")
    total = jnp.sum(jnp.where(upto[:, None, None], everyone, 0.0), axis=0).reshape(both.shape)
    result = jnp.einsum("thi,hij->thj", queries, total, precision=lax.Precision.HIGHEST)
    attended = result[..., :HEAD_DIM] / (result[..., HEAD_DIM:] + EPSILON)
    return attended.astype(jnp.bfloat16).reshape(1, count, -1)


class Layout:
    def __init__(self, mesh):
        self.frames = mesh.shape["frame"]
        self.lows = 2
        self.highs = self.frames // 4

    def pairs(self, target, source=lambda g, hi, b, lo: True):
        out = []
        for g in range(2):
            for hi in range(self.highs):
                for b in range(2):
                    for lo in range(self.lows):
                        if source(g, hi, b, lo):
                            to = target(g, hi, b, lo)
                            out.append((self.place(g, hi, b, lo), self.place(*to)))
        return out

    def place(self, g, hi, b, lo):
        return ((g * self.highs + hi) * 2 + b) * self.lows + lo


def send(a, pairs):
    return lax.ppermute(a, AXES, pairs)


ANY = pl.BlockSpec(memory_space=pl.ANY)
VMEM = pl.BlockSpec(memory_space=pltpu.VMEM)
SMEM = pl.BlockSpec(memory_space=pltpu.SMEM)
LIGHT = pl.CostEstimate(flops=1000, bytes_accessed=1000, transcendentals=0)


def call(body, out, ins, scratch, *operands):
    return pl.pallas_call(
        body,
        out_shape=out,
        in_specs=ins,
        out_specs=jax.tree.map(lambda _: VMEM, out),
        scratch_shapes=scratch,
        compiler_params=pltpu.CompilerParams(vmem_limit_bytes=16 * 2**20),
        cost_estimate=LIGHT,
    )(*operands)


def heads_of(g, width, half):
    shape = (width, width + half)
    row = lax.broadcasted_iota(jnp.int32, shape, 0)
    column = lax.broadcasted_iota(jnp.int32, shape, 1)
    turned = column + half * g
    turned = jnp.where(turned >= width + half, turned - (width + half), turned)
    return (width * g + row) // HEAD_DIM == (4 * half * g + turned) // HEAD_DIM


def pick(place, own, swapped, half):
    width, depth = own.shape[0] // 3, own.shape[1]
    part = -(-depth // 256) * 128
    more = width + half
    rows = 2 * more + width

    def body(place_ref, own_ref, swapped_ref, kv_ref, q_ref, all_ref, other_kv_ref, other_q_ref, full):
        g, lo = place_ref[0], place_ref[3]
        mine = lo == g
        full[:, 2 * part - 128 :] = jnp.zeros((rows, 128), full.dtype)
        at = pl.multiple_of(g * (width - half), 16)
        for start, which in ((0, 1), (more, 2), (more + width, 0)):
            shard = pl.ds(which * width, width)
            full[start : start + width, :depth] = jnp.where(mine, own_ref[shard], swapped_ref[shard])
            if which < 2:
                extra = pl.ds(which * width + at, half)
                full[start + width : start + more, :depth] = jnp.where(mine, swapped_ref[extra], own_ref[extra])
        this = full[:, pl.ds(pl.multiple_of(lo * part, 128), part)]
        that = full[:, pl.ds(pl.multiple_of((1 - lo) * part, 128), part)]
        kv_ref[...] = this[: more + width]
        q_ref[...] = this[more + width :]
        all_ref[...] = this
        other_kv_ref[...] = that[: more + width]
        other_q_ref[...] = that[more + width :]

    shape = lambda n: jax.ShapeDtypeStruct((n, part), own.dtype)
    out = [shape(more + width), shape(more), shape(rows), shape(more + width), shape(more)]
    return call(body, out, [SMEM, VMEM, VMEM], [pltpu.VMEM((rows, 2 * part), own.dtype)], place, own, swapped)


def project(place, half, jobs, blocks, frames, carried=()):
    arrays = []

    def index(a):
        for i, b in enumerate(arrays):
            if a is b:
                return i
        arrays.append(a)
        return len(arrays) - 1

    count = frames[jobs[0][1]][0].shape[1]
    depth = sum(p.shape[0] for p in frames[jobs[0][1]])
    part = blocks[jobs[0][0]][jobs[0][2]][0].shape[1]
    n_q = sum(what == "q" for _, _, what in jobs)
    ms = sorted({m for _, m, what in jobs if what == "kv"} | {m for m, _ in carried})
    more = 3 * HEAD_DIM
    width = more - half
    used = {}
    for k, m, what in jobs:
        one, two, first = blocks[k][what]
        used.setdefault((k, what), (index(one), index(two), first, []))[3].append(m)
    parts = {m: [index(p) for p in frames[m]] for _, m, _ in jobs}
    places, order = {}, []
    for (k, what), (_, _, _, on) in used.items():
        for m in on:
            if what == "q":
                places[k, m] = len(order)
                order.append((k, m))
    n_in = len(arrays)

    def body(place_ref, *refs):
        ins, refs = refs[:n_in], list(refs[n_in:])
        c_refs = [refs.pop(0) for _ in carried]
        q_ref = refs.pop(0) if n_q else None
        s_ref = refs.pop(0) if ms else None
        (w_all,) = refs
        g, lo = place_ref[0], place_ref[3]
        first_half = lo == 0
        if ms:
            same = heads_of(g, width, half)
            ones = jnp.ones((8, count), jnp.bfloat16)
            s_ref[...] = jnp.zeros_like(s_ref)
            for (m, a), c_ref in zip(carried, c_refs):
                s_ref[ms.index(m)] = c_ref[a]
        for i, ((k, what), (one, two, first, on)) in enumerate(used.items()):
            n = more if what == "q" else more + width
            w_ref = w_all.at[i % 2]
            one, two = ins[one][first : first + n], ins[two][first : first + n]
            w_ref[:n, :part] = jnp.where(first_half, one, two)
            w_ref[:n, part:] = jnp.where(first_half, two, one)[:, : depth - part]
            for m in on:
                x = [ins[p][...] for p in parts[m]]
                x = jnp.concatenate(x, axis=0) if len(x) > 1 else x[0]
                made = dot(w_ref[:n], x, ((1,), (0,)))
                if what == "q":
                    q_ref[places[k, m]] = jnp.maximum(made, 0.0)
                    continue
                keys = jnp.maximum(made[:more], 0.0).astype(jnp.bfloat16)
                values = made[more:].astype(jnp.bfloat16)
                full = jnp.where(same, dot(values, keys, ((1,), (1,))), 0.0)
                at = ms.index(m)
                s_ref[at, :width, 32 * k : 32 * k + 32] = full[:, :32] + full[:, 32:64] + full[:, 64:]
                s_ref[at, width + k : width + k + 1, :more] = dot(ones, keys, ((1,), (1,)))[:1]

    out = []
    if n_q:
        out.append(jax.ShapeDtypeStruct((n_q, more, count), jnp.float32))
    if ms:
        out.append(jax.ShapeDtypeStruct((len(ms), width + 16, 128), jnp.float32))
    scratch = [pltpu.VMEM((2, more + width, depth), jnp.bfloat16)]
    ins = [SMEM] + [VMEM] * (n_in + len(carried))
    extra = [a for _, (a, _) in carried]
    carried = [(m, at) for m, (_, at) in carried]
    got = list(call(body, out, ins, scratch, place, *arrays, *extra))
    return ([(order, got.pop(0))] if n_q else []) + ([(ms, got[0])] if ms else [])


def plane_sum(mine, others):
    def body(a_ref, b_ref, out_ref):
        both = a_ref[...] + b_ref[...]
        out_ref[0] = (both[0] + both[1]).astype(out_ref.dtype)
        out_ref[1] = (both[2] + both[3]).astype(out_ref.dtype)

    out = jax.ShapeDtypeStruct((2,) + mine.shape[1:], jnp.bfloat16)
    return call(body, out, [VMEM] * 2, [], mine, others)


def apply(place, half, ms, queries, mine, others, planes):
    arrays = []
    where = {}
    for m in ms:
        for k in range(4):
            a, at = queries[k, m]
            if not any(a is b for b in arrays):
                arrays.append(a)
            where[k, m] = ([a is b for b in arrays].index(True), at)
    rows, count = arrays[0].shape[1:]
    width = rows - half

    def body(place_ref, *refs):
        q_refs = refs[: len(arrays)]
        mine_ref, others_ref, *plane_refs = refs[len(arrays) : len(arrays) + 5]
        outs = refs[len(arrays) + 5 :]
        g, hi, b, lo = (place_ref[i] for i in range(4))
        same = heads_of(g, width, half)
        factor = lambda yes: jnp.where(yes, 1.0, 0.0).astype(jnp.float32)
        earlier = [factor(jnp.bitwise_xor(hi, k) < hi) for k in (1, 2, 3)]
        second = factor(lo == 1)

        def split(a):
            high = a.astype(jnp.bfloat16)
            return high, (a - high.astype(jnp.float32)).astype(jnp.bfloat16)

        for out_ref, m in zip(outs, ms):
            after = factor(jnp.bitwise_xor(b, m & 1) == 1)
            upto = mine_ref[m] + second * others_ref[m] + after * (mine_ref[m ^ 1] + others_ref[m ^ 1])
            before = [earlier[i] * plane_refs[i][m // 2].astype(jnp.float32) for i in range(3)]
            for j in range(4):
                part = upto[:width, 32 * j : 32 * j + 32]
                sums = upto[width + j : width + j + 1, :rows]
                for k in (1, 2, 3):
                    i = j ^ k
                    part += before[k - 1][:width, 32 * i : 32 * i + 32]
                    sums += before[k - 1][width + i : width + i + 1, :rows]
                state = jnp.where(same, jnp.concatenate([part] * 3, axis=1), 0.0)
                sums = jnp.where(same, jnp.broadcast_to(sums, (width, rows)), 0.0)
                left, left_low = split(jnp.concatenate([state, sums], axis=0))
                a, at = where[j, m]
                q, q_low = split(q_refs[a][at])
                both = dot(left, q, ((1,), (0,))) + dot(left_low, q, ((1,), (0,))) + dot(left, q_low, ((1,), (0,)))
                out_ref[j] = (both[:width] / (both[width:] + EPSILON)).astype(jnp.bfloat16)

    out = [jax.ShapeDtypeStruct((4, width, count), jnp.bfloat16)] * len(ms)
    ins = [SMEM] + [VMEM] * (len(arrays) + 5)
    return call(body, out, ins, [], place, *arrays, mine, others, *planes)


def assemble(place, got):
    blocks, width, count = got[0].shape

    def body(place_ref, *refs):
        *got_refs, out_ref, every = refs
        g, hi, b = (place_ref[i] for i in range(3))
        for m in range(4):
            this_g, this_b = jnp.bitwise_xor(g, m >> 1), jnp.bitwise_xor(b, m & 1)
            for k in range(blocks):
                at = ((jnp.bitwise_xor(hi, k) * 2 + this_b) * 2 + this_g) * width
                every[pl.ds(pl.multiple_of(at, 16), width)] = got_refs[m][k]
        out_ref[...] = every[...].T

    out = jax.ShapeDtypeStruct((count, 4 * blocks * width), jnp.bfloat16)
    scratch = [pltpu.VMEM((4 * blocks * width, count), jnp.bfloat16)]
    return call(body, out, [SMEM] + [VMEM] * 4, scratch, place, *got)


def shared_plan(layout, frames_in, qkv_weight):
    g = lax.axis_index("groups")
    frame = lax.axis_index("frame")
    lo, b, hi = frame % 2, (frame // 2) % 2, frame // 4
    place = jnp.stack([g, hi, b, lo]).astype(jnp.int32)
    weights = qkv_weight.transpose(0, 2, 1)
    width, depth = weights.shape[1:]
    half = HEAD_DIM // 2
    own = frames_in[0].T

    along = lambda k: layout.pairs(lambda g, hi, b, lo: (g, hi ^ k, b, lo))
    over_b = layout.pairs(lambda g, hi, b, lo: (g, hi, 1 - b, lo))
    over_g = layout.pairs(lambda g, hi, b, lo: (1 - g, hi, b, lo))
    over_gb = layout.pairs(lambda g, hi, b, lo: (1 - g, hi, 1 - b, lo))
    over_lo = layout.pairs(lambda g, hi, b, lo: (g, hi, b, 1 - lo))

    next_b = send(own, over_b)
    next_g = send(own, over_g)

    shard = weights.reshape(3 * width, depth)
    kv, q, whole, other_kv, other_q = pick(place, shard, send(shard, over_lo), half)
    far_kv = send(kv, along(2))
    far_q = send(q, along(2))
    near = send(whole, along(1))
    last_kv = send(far_kv, along(1))
    far_kv, far_q, last_kv, next_b, next_g = lax.optimization_barrier((far_kv, far_q, last_kv, next_b, next_g))
    last_q = send(far_q, along(1))

    cut = depth // 2
    across = [send(next_b[:cut], over_g), send(next_g[cut:], over_b)]
    frames = [[own], [next_b], [next_g], across]

    near_other = send(near, over_lo)
    kv_rows = kv.shape[0]
    blocks = [
        {"kv": (kv, other_kv, 0), "q": (q, other_q, 0)},
        {"kv": (near, near_other, 0), "q": (near, near_other, kv_rows)},
        {"kv": (far_kv, send(far_kv, over_lo), 0), "q": (far_q, send(far_q, over_lo), 0)},
        {"kv": (last_kv, send(last_kv, over_lo), 0), "q": (last_q, send(last_q, over_lo), 0)},
    ]
    queries = {}

    def keep(made):
        order, array = made
        queries.update({km: (array, at) for at, km in enumerate(order)})

    early = [(k, m, what) for k in range(3) for what in ("kv", "q") for m in range(3)]
    made, (_, states) = project(place, half, early, blocks, frames)
    keep(made)
    late = [(3, m, "kv") for m in range(3)] + [(k, 3, "kv") for k in range(4)]
    ((_, mine),) = project(place, half, late, blocks, frames, [(m, (states, m)) for m in range(3)])
    others = send(mine, over_lo)
    plane = plane_sum(mine, others)
    planes = [send(plane, along(k)) for k in (1, 2, 3)]
    last = [(k, 3, "q") for k in range(4)] + [(3, m, "q") for m in range(3)]
    (made,) = project(place, half, last, blocks, frames)
    keep(made)

    out1, out2, out3 = apply(place, half, [1, 2, 3], queries, mine, others, planes)
    (out0,) = apply(place, half, [0], queries, mine, others, planes)
    got = [out0, send(out1, over_b), send(out2, over_g), send(out3, over_gb)]
    return assemble(place, got)[None]


def solution(mesh):
    placed = (P(AXES, None, None), P(None, None, "frame"))

    def shards(frames_in, qkv_weight):
        width = qkv_weight.shape[2]
        if mesh.shape["groups"] == 2 and mesh.shape["frame"] == 16 and width * 2 == 5 * HEAD_DIM:
            return shared_plan(Layout(mesh), frames_in, qkv_weight)
        return gathered_plan(frames_in, qkv_weight)

    return jax.shard_map(
        shards, mesh=mesh, in_specs=placed, out_specs=P(AXES, None, None), check_vma=False
    )
```

```python
import jax
import jax.numpy as jnp
from jax import lax
from jax.experimental import pallas as pl
from jax.experimental.pallas import tpu as pltpu
from jax.sharding import PartitionSpec as P

HEAD_DIM = 32
EPSILON = 1e-06
AXES = ("groups", "frame")


def dot(a, b, dims):
    return lax.dot_general(a, b, (dims, ((), ())), preferred_element_type=jnp.float32)


def gathered_plan(frames_in, qkv_weight):
    tokens = frames_in[0]
    count = tokens.shape[0]
    weights = lax.all_gather(qkv_weight, "frame", axis=2, tiled=True)
    projected = jnp.einsum("td,sdc->stc", tokens, weights, preferred_element_type=jnp.float32)
    heads = weights.shape[2] // HEAD_DIM
    split = lambda a: a.reshape(count, heads, HEAD_DIM)
    queries = split(jax.nn.relu(projected[0]))
    keys = split(jax.nn.relu(projected[1].astype(jnp.bfloat16)))
    values = split(projected[2].astype(jnp.bfloat16))
    state = jnp.einsum("thi,thj->hij", keys, values, preferred_element_type=jnp.float32)
    key_sum = jnp.sum(keys.astype(jnp.float32), axis=0)
    both = jnp.concatenate([state, key_sum[:, :, None]], axis=2)
    everyone = lax.all_gather(both.reshape(heads, -1), "frame")
    upto = jnp.arange(everyone.shape[0]) <= lax.axis_index("frame")
    total = jnp.sum(jnp.where(upto[:, None, None], everyone, 0.0), axis=0).reshape(both.shape)
    result = jnp.einsum("thi,hij->thj", queries, total, precision=lax.Precision.HIGHEST)
    attended = result[..., :HEAD_DIM] / (result[..., HEAD_DIM:] + EPSILON)
    return attended.astype(jnp.bfloat16).reshape(1, count, -1)


class Layout:
    def __init__(self, mesh):
        self.frames = mesh.shape["frame"]
        self.lows = 2
        self.highs = self.frames // 4

    def pairs(self, target, source=lambda g, hi, b, lo: True):
        out = []
        for g in range(2):
            for hi in range(self.highs):
                for b in range(2):
                    for lo in range(self.lows):
                        if source(g, hi, b, lo):
                            to = target(g, hi, b, lo)
                            out.append((self.place(g, hi, b, lo), self.place(*to)))
        return out

    def place(self, g, hi, b, lo):
        return ((g * self.highs + hi) * 2 + b) * self.lows + lo


def send(a, pairs):
    return lax.ppermute(a, AXES, pairs)


ANY = pl.BlockSpec(memory_space=pl.ANY)
VMEM = pl.BlockSpec(memory_space=pltpu.VMEM)
SMEM = pl.BlockSpec(memory_space=pltpu.SMEM)
LIGHT = pl.CostEstimate(flops=1000, bytes_accessed=1000, transcendentals=0)


def call(body, out, ins, scratch, *operands):
    return pl.pallas_call(
        body,
        out_shape=out,
        in_specs=ins,
        out_specs=jax.tree.map(lambda _: VMEM, out),
        scratch_shapes=scratch,
        compiler_params=pltpu.CompilerParams(vmem_limit_bytes=16 * 2**20),
        cost_estimate=LIGHT,
    )(*operands)


def heads_of(g, width, half):
    shape = (width, width + half)
    row = lax.broadcasted_iota(jnp.int32, shape, 0)
    column = lax.broadcasted_iota(jnp.int32, shape, 1)
    turned = column + half * g
    turned = jnp.where(turned >= width + half, turned - (width + half), turned)
    return (width * g + row) // HEAD_DIM == (4 * half * g + turned) // HEAD_DIM


def pick(place, own, swapped, half):
    width, depth = own.shape[0] // 3, own.shape[1]
    part = -(-depth // 256) * 128
    more = width + half
    rows = 2 * more + width
    chunks = [pl.ds(width * i, width) for i in range(3)]

    def body(place_ref, own_hbm, swapped_ref, kv_ref, q_ref, all_ref, other_kv_ref, other_q_ref, full, own_ref, sems):
        reads = [pltpu.make_async_copy(own_hbm.at[r], own_ref.at[r], sems.at[i]) for i, r in enumerate(chunks)]
        for read in reads:
            read.start()
        g, lo = place_ref[0], place_ref[3]
        mine = lo == g
        full[:, 2 * part - 128 :] = jnp.zeros((rows, 128), full.dtype)
        at = pl.multiple_of(g * (width - half), 16)
        for read in reads:
            read.wait()
        for start, which in ((0, 1), (more, 2), (more + width, 0)):
            shard = pl.ds(which * width, width)
            full[start : start + width, :depth] = jnp.where(mine, own_ref[shard], swapped_ref[shard])
            if which < 2:
                extra = pl.ds(which * width + at, half)
                full[start + width : start + more, :depth] = jnp.where(mine, swapped_ref[extra], own_ref[extra])
        this = full[:, pl.ds(pl.multiple_of(lo * part, 128), part)]
        that = full[:, pl.ds(pl.multiple_of((1 - lo) * part, 128), part)]
        kv_ref[...] = this[: more + width]
        q_ref[...] = this[more + width :]
        all_ref[...] = this
        other_kv_ref[...] = that[: more + width]
        other_q_ref[...] = that[more + width :]

    shape = lambda n: jax.ShapeDtypeStruct((n, part), own.dtype)
    out = [shape(more + width), shape(more), shape(rows), shape(more + width), shape(more)]
    scratch = [
        pltpu.VMEM((rows, 2 * part), own.dtype),
        pltpu.VMEM(own.shape, own.dtype),
        pltpu.SemaphoreType.DMA((len(chunks),)),
    ]
    return call(body, out, [SMEM, ANY, VMEM], scratch, place, own, swapped)


def project(place, half, jobs, blocks, frames, carried=(), keep=False, given=None):
    arrays, pieces, rows = [], {}, 0

    def index(a):
        for i, b in enumerate(arrays):
            if a is b:
                return i
        arrays.append(a)
        return len(arrays) - 1

    more = 3 * HEAD_DIM
    width = more - half
    tall = {"kv": more + width, "q": more}
    for named, ms in jobs:
        for k, what in named:
            if (k, what) not in pieces:
                chunks = [(index(one), index(two), *at) for one, two, *at in blocks[k][what]]
                pieces[k, what] = (chunks, rows)
                rows += tall[what]
    if given is not None:
        pieces, rows = given[0], 0
    parts = {m: [index(p) for p in frames[m]] for _, ms in jobs for m in ms}
    count = frames[0][0].shape[1]
    depth = frames[0][0].shape[0]
    part = arrays[0].shape[1]
    if given is not None:
        arrays = [given[1]]
        parts = {m: [index(p) for p in frames[m]] for _, ms in jobs for m in ms}
    held = sorted({m for named, ms in jobs for m in ms if any(w == "kv" for _, w in named)} | {m for m, _, _ in carried})
    places = {}
    for named, ms in jobs:
        for m in ms:
            for k, what in named:
                if what == "q":
                    places[k, m] = len(places)
    n_in = len(arrays)

    def body(place_ref, *refs):
        ins, refs = refs[:n_in], list(refs[n_in:])
        c_refs = [refs.pop(0) for _ in carried]
        q_ref = refs.pop(0) if places else None
        s_ref = refs.pop(0) if held else None
        w_ref = refs.pop(0) if given is None else ins[0]
        g, lo = place_ref[0], place_ref[3]
        first_half = lo == 0
        if held:
            same = heads_of(g, width, half)
            ones = jnp.ones((8, count), jnp.bfloat16)
            s_ref[...] = jnp.zeros_like(s_ref)
            for (m, _, at), c_ref in zip(carried, c_refs):
                s_ref[held.index(m)] = c_ref[at]
        for chunks, at in [] if given is not None else pieces.values():
            for one, two, first, second, n in chunks:
                one, two = ins[one][first : first + n], ins[two][second : second + n]
                w_ref[at : at + n, :part] = jnp.where(first_half, one, two)
                w_ref[at : at + n, part:] = jnp.where(first_half, two, one)[:, : depth - part]
                at += n
        for named, ms in jobs:
            start = pieces[named[0]][1]
            stop = pieces[named[-1]][1] + tall[named[-1][1]]
            for m in ms:
                x = [ins[p][...] for p in parts[m]]
                x = jnp.concatenate(x, axis=0) if len(x) > 1 else x[0]
                all_made = dot(w_ref[start:stop], x, ((1,), (0,)))
                for k, what in named:
                    at = pieces[k, what][1] - start
                    made = all_made[at : at + tall[what]]
                    if what == "q":
                        q_ref[places[k, m]] = jnp.maximum(made, 0.0)
                        continue
                    keys = jnp.maximum(made[:more], 0.0).astype(jnp.bfloat16)
                    values = made[more:].astype(jnp.bfloat16)
                    full = jnp.where(same, dot(values, keys, ((1,), (1,))), 0.0)
                    at = held.index(m)
                    s_ref[at, :width, 32 * k : 32 * k + 32] = full[:, :32] + full[:, 32:64] + full[:, 64:]
                    s_ref[at, width + k : width + k + 1, :more] = dot(ones, keys, ((1,), (1,)))[:1]

    out = []
    if places:
        out.append(jax.ShapeDtypeStruct((len(places), more, count), jnp.float32))
    if held:
        out.append(jax.ShapeDtypeStruct((len(held), width + 16, 128), jnp.float32))
    scratch = []
    if keep:
        out.append(jax.ShapeDtypeStruct((rows, depth), jnp.bfloat16))
    elif given is None:
        scratch.append(pltpu.VMEM((rows, depth), jnp.bfloat16))
    ins = [SMEM] + [VMEM] * (n_in + len(carried))
    got = list(call(body, out, ins, scratch, place, *arrays, *[a for _, a, _ in carried]))
    made = ([(places, got.pop(0))] if places else []) + ([(held, got.pop(0))] if held else [])
    return made + ([(pieces, got[0])] if keep else [])


def plane_sum(mine, others):
    def body(a_ref, b_ref, out_ref):
        both = a_ref[...] + b_ref[...]
        out_ref[0] = (both[0] + both[1]).astype(out_ref.dtype)
        out_ref[1] = (both[2] + both[3]).astype(out_ref.dtype)

    out = jax.ShapeDtypeStruct((2,) + mine.shape[1:], jnp.bfloat16)
    return call(body, out, [VMEM] * 2, [], mine, others)


def turn(a, k):
    lanes = [a[..., 32 * (j ^ k) : 32 * (j ^ k) + 32] for j in range(4)]
    rows = a.shape[-2] - 16
    sums = [a[..., rows + (j ^ k) : rows + (j ^ k) + 1, :] for j in range(4)]
    return jnp.concatenate([jnp.concatenate(lanes, axis=-1)[..., :rows, :], *sums, a[..., rows + 4 :, :]], axis=-2)


def pair_sum(plane, near):
    def body(a_ref, b_ref, out_ref):
        for i in range(2):
            both = a_ref[i].astype(jnp.float32) + turn(b_ref[i].astype(jnp.float32), 1)
            out_ref[i] = both.astype(out_ref.dtype)

    return call(body, jax.ShapeDtypeStruct(plane.shape, plane.dtype), [VMEM] * 2, [], plane, near)


def apply(place, half, ms, queries, mine, others, planes):
    arrays = []
    where = {}
    for m in ms:
        for k in range(4):
            a, at = queries[k, m]
            if not any(a is b for b in arrays):
                arrays.append(a)
            where[k, m] = ([a is b for b in arrays].index(True), at)
    rows, count = arrays[0].shape[1:]
    width = rows - half

    def body(place_ref, *refs):
        q_refs = refs[: len(arrays)]
        mine_ref, others_ref = refs[len(arrays) : len(arrays) + 2]
        plane_refs, outs = refs[len(arrays) + 2 : -len(ms)], refs[-len(ms) :]
        g, hi, b, lo = (place_ref[i] for i in range(4))
        same = heads_of(g, width, half)
        factor = lambda yes: jnp.where(yes, 1.0, 0.0).astype(jnp.float32)
        second = factor(lo == 1)

        def split(a):
            high = a.astype(jnp.bfloat16)
            return high, (a - high.astype(jnp.float32)).astype(jnp.bfloat16)

        for out_ref, m in zip(outs, ms):
            after = factor(jnp.bitwise_xor(b, m & 1) == 1)
            upto = mine_ref[m] + second * others_ref[m] + after * (mine_ref[m ^ 1] + others_ref[m ^ 1])
            for ref, (_, k, adds) in zip(plane_refs, planes):
                upto += factor(adds(hi)) * turn(ref[m // 2].astype(jnp.float32), k)
            for j in range(4):
                part = upto[:width, 32 * j : 32 * j + 32]
                sums = upto[width + j : width + j + 1, :rows]
                state = jnp.where(same, jnp.concatenate([part] * 3, axis=1), 0.0)
                sums = jnp.where(same, jnp.broadcast_to(sums, (width, rows)), 0.0)
                left, left_low = split(jnp.concatenate([state, sums], axis=0))
                a, at = where[j, m]
                q, q_low = split(q_refs[a][at])
                both = dot(left, q, ((1,), (0,))) + dot(left_low, q, ((1,), (0,))) + dot(left, q_low, ((1,), (0,)))
                out_ref[j] = (both[:width] / (both[width:] + EPSILON)).astype(jnp.bfloat16)

    out = [jax.ShapeDtypeStruct((4, width, count), jnp.bfloat16)] * len(ms)
    ins = [SMEM] + [VMEM] * (len(arrays) + 2 + len(planes))
    return call(body, out, ins, [], place, *arrays, mine, others, *[p for p, _, _ in planes])


def assemble(place, got):
    blocks, width, count = got[0].shape

    def body(place_ref, *refs):
        *got_refs, out_ref, every = refs
        g, hi, b = (place_ref[i] for i in range(3))
        for m in range(4):
            this_g, this_b = jnp.bitwise_xor(g, m >> 1), jnp.bitwise_xor(b, m & 1)
            for k in range(blocks):
                at = ((jnp.bitwise_xor(hi, k) * 2 + this_b) * 2 + this_g) * width
                every[pl.ds(pl.multiple_of(at, 16), width)] = got_refs[m][k]
        out_ref[...] = every[...].T

    out = jax.ShapeDtypeStruct((count, 4 * blocks * width), jnp.bfloat16)
    scratch = [pltpu.VMEM((4 * blocks * width, count), jnp.bfloat16)]
    return call(body, out, [SMEM] + [VMEM] * 4, scratch, place, *got)


def shared_plan(layout, frames_in, qkv_weight):
    g = lax.axis_index("groups")
    frame = lax.axis_index("frame")
    lo, b, hi = frame % 2, (frame // 2) % 2, frame // 4
    place = jnp.stack([g, hi, b, lo]).astype(jnp.int32)
    weights = qkv_weight.transpose(0, 2, 1)
    width, depth = weights.shape[1:]
    half = HEAD_DIM // 2
    own = frames_in[0].T

    along = lambda k: layout.pairs(lambda g, hi, b, lo: (g, hi ^ k, b, lo))
    over_b = layout.pairs(lambda g, hi, b, lo: (g, hi, 1 - b, lo))
    over_g = layout.pairs(lambda g, hi, b, lo: (1 - g, hi, b, lo))
    over_gb = layout.pairs(lambda g, hi, b, lo: (1 - g, hi, 1 - b, lo))
    over_lo = layout.pairs(lambda g, hi, b, lo: (g, hi, b, 1 - lo))

    next_b = send(own, over_b)
    next_g = send(own, over_g)
    shard = weights.reshape(3 * width, depth)
    kv, q, whole, other_kv, other_q = pick(place, shard, send(shard, over_lo), half)
    more, kv_rows = q.shape[0], kv.shape[0]
    queries = {}

    def keep(made):
        places, array = made
        queries.update({km: (array, at) for km, at in places.items()})

    def swapped(a, first=0, rows=None):
        if rows is None:
            return [(a, send(a, over_lo), 0, 0, a.shape[0])]
        return [(a, send(a[first : first + rows], over_lo), first, 0, rows)]

    far_kv = send(kv, along(2))
    far_q = send(q, along(2))
    near = send(whole, along(1))
    next_b, next_g = lax.optimization_barrier((next_b, next_g))
    last_kv = send(far_kv, along(1))
    cut = depth // 2
    across = [send(next_b[:cut], over_g), send(next_g[cut:], over_b)]
    frames = [[own], [next_b], [next_g], across]
    blocks = [{"kv": [(kv, other_kv, 0, 0, kv_rows)], "q": [(q, other_q, 0, 0, more)]} for _ in range(4)]
    blocks[2]["kv"] = swapped(far_kv)
    blocks[1]["kv"] = swapped(near, 0, kv_rows)
    jobs = [([(k, "kv") for k in range(3)] + [(0, "q")], [0, 1, 2])]
    made, (_, states), given = project(place, half, jobs, blocks, frames, keep=True)
    keep(made)
    *across, states = lax.optimization_barrier((*across, states))
    frames[3] = across
    ((_, states_3),) = project(place, half, [([(k, "kv") for k in range(3)], [3])], blocks, frames, given=given)
    last_kv, states_3 = lax.optimization_barrier((last_kv, states_3))
    blocks[3]["kv"] = swapped(last_kv)
    last_q = send(far_q, along(1))
    blocks[2]["q"], blocks[3]["q"] = swapped(far_q), swapped(last_q)
    blocks[1]["q"] = swapped(near, kv_rows, more)
    carried = [(m, states, m) for m in range(3)] + [(3, states_3, 0)]
    ((_, mine),) = project(place, half, [([(3, "kv")], [0, 1, 2, 3])], blocks, frames, carried)
    others = send(mine, over_lo)
    plane = plane_sum(mine, others)
    planes = [(send(plane, along(k)), k, lambda hi, k=k: jnp.bitwise_xor(hi, k) < hi) for k in (1, 2, 3)]
    last = [([(k, "q") for k in range(4)], [3]), ([(k, "q") for k in (1, 2, 3)], [0, 1, 2])]
    (made,) = project(place, half, last, blocks, frames)
    keep(made)

    out1, out2, out3 = apply(place, half, [1, 2, 3], queries, mine, others, planes)
    (out0,) = apply(place, half, [0], queries, mine, others, planes)
    out1 = send(out1, over_b)
    out2 = send(out2, over_g)
    out3 = send(out3, over_gb)
    return assemble(place, [out0, out1, out2, out3])[None]


def solution(mesh):
    placed = (P(AXES, None, None), P(None, None, "frame"))

    def shards(frames_in, qkv_weight):
        width = qkv_weight.shape[2]
        if mesh.shape["groups"] == 2 and mesh.shape["frame"] == 16 and width * 2 == 5 * HEAD_DIM:
            return shared_plan(Layout(mesh), frames_in, qkv_weight)
        return gathered_plan(frames_in, qkv_weight)

    return jax.shard_map(
        shards, mesh=mesh, in_specs=placed, out_specs=P(AXES, None, None), check_vma=False
    )
```

```python
import jax
import jax.numpy as jnp
from jax import lax
from jax.experimental import pallas as pl
from jax.experimental.pallas import tpu as pltpu
from jax.sharding import PartitionSpec as P

HEAD_DIM = 32
EPSILON = 1e-06
AXES = ("groups", "frame")


def dot(a, b, dims):
    return lax.dot_general(a, b, (dims, ((), ())), preferred_element_type=jnp.float32)


def gathered_plan(frames_in, qkv_weight):
    tokens = frames_in[0]
    count = tokens.shape[0]
    weights = lax.all_gather(qkv_weight, "frame", axis=2, tiled=True)
    projected = jnp.einsum("td,sdc->stc", tokens, weights, preferred_element_type=jnp.float32)
    heads = weights.shape[2] // HEAD_DIM
    split = lambda a: a.reshape(count, heads, HEAD_DIM)
    queries = split(jax.nn.relu(projected[0]))
    keys = split(jax.nn.relu(projected[1].astype(jnp.bfloat16)))
    values = split(projected[2].astype(jnp.bfloat16))
    state = jnp.einsum("thi,thj->hij", keys, values, preferred_element_type=jnp.float32)
    key_sum = jnp.sum(keys.astype(jnp.float32), axis=0)
    both = jnp.concatenate([state, key_sum[:, :, None]], axis=2)
    everyone = lax.all_gather(both.reshape(heads, -1), "frame")
    upto = jnp.arange(everyone.shape[0]) <= lax.axis_index("frame")
    total = jnp.sum(jnp.where(upto[:, None, None], everyone, 0.0), axis=0).reshape(both.shape)
    result = jnp.einsum("thi,hij->thj", queries, total, precision=lax.Precision.HIGHEST)
    attended = result[..., :HEAD_DIM] / (result[..., HEAD_DIM:] + EPSILON)
    return attended.astype(jnp.bfloat16).reshape(1, count, -1)


class Layout:
    def __init__(self, mesh):
        self.frames = mesh.shape["frame"]
        self.lows = 2
        self.highs = self.frames // 4

    def pairs(self, target, source=lambda g, hi, b, lo: True):
        out = []
        for g in range(2):
            for hi in range(self.highs):
                for b in range(2):
                    for lo in range(self.lows):
                        if source(g, hi, b, lo):
                            to = target(g, hi, b, lo)
                            out.append((self.place(g, hi, b, lo), self.place(*to)))
        return out

    def place(self, g, hi, b, lo):
        return ((g * self.highs + hi) * 2 + b) * self.lows + lo


def send(a, pairs):
    return lax.ppermute(a, AXES, pairs)


ANY = pl.BlockSpec(memory_space=pl.ANY)
VMEM = pl.BlockSpec(memory_space=pltpu.VMEM)
LIGHT = pl.CostEstimate(flops=1000, bytes_accessed=1000, transcendentals=0)


def position():
    frame = lax.axis_index("frame")
    return lax.axis_index("groups"), frame // 4, (frame // 2) % 2, frame % 2


def call(body, out, ins, scratch, *operands):
    return pl.pallas_call(
        body,
        out_shape=out,
        in_specs=ins,
        out_specs=jax.tree.map(lambda _: VMEM, out),
        scratch_shapes=scratch,
        compiler_params=pltpu.CompilerParams(vmem_limit_bytes=16 * 2**20),
        cost_estimate=LIGHT,
    )(*operands)


def heads_of(g, width, half):
    shape = (width, width + half)
    row = lax.broadcasted_iota(jnp.int32, shape, 0)
    column = lax.broadcasted_iota(jnp.int32, shape, 1)
    turned = column + half * g
    turned = jnp.where(turned >= width + half, turned - (width + half), turned)
    return (width * g + row) // HEAD_DIM == (4 * half * g + turned) // HEAD_DIM


def pick(own, swapped, half):
    width, depth = own.shape[0] // 3, own.shape[1]
    part = -(-depth // 256) * 128
    more = width + half
    rows = 2 * more + width

    def body(own_ref, swapped_ref, kv_ref, q_ref, all_ref, other_kv_ref, other_q_ref, full):
        g, _, _, lo = position()
        mine = lo == g
        full[:, 2 * part - 128 :] = jnp.zeros((rows, 128), full.dtype)
        at = pl.multiple_of(g * (width - half), 16)
        for start, which in ((0, 1), (more, 2), (more + width, 0)):
            shard = pl.ds(which * width, width)
            full[start : start + width, :depth] = jnp.where(mine, own_ref[shard], swapped_ref[shard])
            if which < 2:
                extra = pl.ds(which * width + at, half)
                full[start + width : start + more, :depth] = jnp.where(mine, swapped_ref[extra], own_ref[extra])
        this = full[:, pl.ds(pl.multiple_of(lo * part, 128), part)]
        that = full[:, pl.ds(pl.multiple_of((1 - lo) * part, 128), part)]
        kv_ref[...] = this[: more + width]
        q_ref[...] = this[more + width :]
        all_ref[...] = this
        other_kv_ref[...] = that[: more + width]
        other_q_ref[...] = that[more + width :]

    shape = lambda n: jax.ShapeDtypeStruct((n, part), own.dtype)
    out = [shape(more + width), shape(more), shape(rows), shape(more + width), shape(more)]
    return call(body, out, [VMEM, VMEM], [pltpu.VMEM((rows, 2 * part), own.dtype)], own, swapped)


def project(half, jobs, blocks, frames, carried=(), keep=False, given=None):
    arrays, pieces, rows = [], {}, 0

    def index(a):
        for i, b in enumerate(arrays):
            if a is b:
                return i
        arrays.append(a)
        return len(arrays) - 1

    more = 3 * HEAD_DIM
    width = more - half
    tall = {"kv": more + width, "q": more}
    for named, ms in jobs:
        for k, what in named:
            if (k, what) not in pieces:
                chunks = [(index(one), index(two), *at) for one, two, *at in blocks[k][what]]
                pieces[k, what] = (chunks, rows)
                rows += tall[what]
    if given is not None:
        pieces, rows = given[0], 0
    parts = {m: [index(p) for p in frames[m]] for _, ms in jobs for m in ms}
    count = frames[0][0].shape[1]
    depth = frames[0][0].shape[0]
    part = arrays[0].shape[1]
    if given is not None:
        arrays = [given[1]]
        parts = {m: [index(p) for p in frames[m]] for _, ms in jobs for m in ms}
    held = sorted({m for named, ms in jobs for m in ms if any(w == "kv" for _, w in named)} | {m for m, _, _ in carried})
    places = {}
    for named, ms in jobs:
        for m in ms:
            for k, what in named:
                if what == "q":
                    places[k, m] = len(places)
    n_in = len(arrays)

    def body(*refs):
        ins, refs = refs[:n_in], list(refs[n_in:])
        c_refs = [refs.pop(0) for _ in carried]
        q_ref = refs.pop(0) if places else None
        s_ref = refs.pop(0) if held else None
        w_ref = refs.pop(0) if given is None else ins[0]
        g, _, _, lo = position()
        first_half = lo == 0
        if held:
            same = heads_of(g, width, half)
            ones = jnp.ones((8, count), jnp.bfloat16)
            s_ref[...] = jnp.zeros_like(s_ref)
            for (m, _, at), c_ref in zip(carried, c_refs):
                s_ref[held.index(m)] = c_ref[at]
        for chunks, at in [] if given is not None else pieces.values():
            for one, two, first, second, n in chunks:
                one, two = ins[one][first : first + n], ins[two][second : second + n]
                w_ref[at : at + n, :part] = jnp.where(first_half, one, two)
                w_ref[at : at + n, part:] = jnp.where(first_half, two, one)[:, : depth - part]
                at += n
        for named, ms in jobs:
            start = pieces[named[0]][1]
            stop = pieces[named[-1]][1] + tall[named[-1][1]]
            for m in ms:
                x = [ins[p][...] for p in parts[m]]
                x = jnp.concatenate(x, axis=0) if len(x) > 1 else x[0]
                all_made = dot(w_ref[start:stop], x, ((1,), (0,)))
                for k, what in named:
                    at = pieces[k, what][1] - start
                    made = all_made[at : at + tall[what]]
                    if what == "q":
                        q_ref[places[k, m]] = jnp.maximum(made, 0.0)
                        continue
                    keys = jnp.maximum(made[:more], 0.0).astype(jnp.bfloat16)
                    values = made[more:].astype(jnp.bfloat16)
                    full = jnp.where(same, dot(values, keys, ((1,), (1,))), 0.0)
                    at = held.index(m)
                    s_ref[at, :width, 32 * k : 32 * k + 32] = full[:, :32] + full[:, 32:64] + full[:, 64:]
                    s_ref[at, width + k : width + k + 1, :more] = dot(ones, keys, ((1,), (1,)))[:1]

    out = []
    if places:
        out.append(jax.ShapeDtypeStruct((len(places), more, count), jnp.float32))
    if held:
        out.append(jax.ShapeDtypeStruct((len(held), width + 16, 128), jnp.float32))
    scratch = []
    if keep:
        out.append(jax.ShapeDtypeStruct((rows, depth), jnp.bfloat16))
    elif given is None:
        scratch.append(pltpu.VMEM((rows, depth), jnp.bfloat16))
    ins = [VMEM] * (n_in + len(carried))
    got = list(call(body, out, ins, scratch, *arrays, *[a for _, a, _ in carried]))
    made = ([(places, got.pop(0))] if places else []) + ([(held, got.pop(0))] if held else [])
    return made + ([(pieces, got[0])] if keep else [])


def plane_sum(mine, others):
    def body(a_ref, b_ref, out_ref):
        both = a_ref[...] + b_ref[...]
        out_ref[0] = (both[0] + both[1]).astype(out_ref.dtype)
        out_ref[1] = (both[2] + both[3]).astype(out_ref.dtype)

    out = jax.ShapeDtypeStruct((2,) + mine.shape[1:], jnp.bfloat16)
    return call(body, out, [VMEM] * 2, [], mine, others)


def turn(a, k):
    lanes = [a[..., 32 * (j ^ k) : 32 * (j ^ k) + 32] for j in range(4)]
    rows = a.shape[-2] - 16
    sums = [a[..., rows + (j ^ k) : rows + (j ^ k) + 1, :] for j in range(4)]
    return jnp.concatenate([jnp.concatenate(lanes, axis=-1)[..., :rows, :], *sums, a[..., rows + 4 :, :]], axis=-2)


def pair_sum(plane, near):
    def body(a_ref, b_ref, out_ref):
        for i in range(2):
            both = a_ref[i].astype(jnp.float32) + turn(b_ref[i].astype(jnp.float32), 1)
            out_ref[i] = both.astype(out_ref.dtype)

    return call(body, jax.ShapeDtypeStruct(plane.shape, plane.dtype), [VMEM] * 2, [], plane, near)


def apply(half, ms, queries, mine, others, planes):
    arrays = []
    where = {}
    for m in ms:
        for k in range(4):
            a, at = queries[k, m]
            if not any(a is b for b in arrays):
                arrays.append(a)
            where[k, m] = ([a is b for b in arrays].index(True), at)
    rows, count = arrays[0].shape[1:]
    width = rows - half

    def body(*refs):
        q_refs = refs[: len(arrays)]
        mine_ref, others_ref = refs[len(arrays) : len(arrays) + 2]
        plane_refs, outs = refs[len(arrays) + 2 : -len(ms)], refs[-len(ms) :]
        g, hi, b, lo = position()
        same = heads_of(g, width, half)
        factor = lambda yes: jnp.where(yes, 1.0, 0.0).astype(jnp.float32)
        second = factor(lo == 1)

        def split(a):
            high = a.astype(jnp.bfloat16)
            return high, (a - high.astype(jnp.float32)).astype(jnp.bfloat16)

        for out_ref, m in zip(outs, ms):
            after = factor(jnp.bitwise_xor(b, m & 1) == 1)
            upto = mine_ref[m] + second * others_ref[m] + after * (mine_ref[m ^ 1] + others_ref[m ^ 1])
            for ref, (_, k, adds) in zip(plane_refs, planes):
                upto += factor(adds(hi)) * turn(ref[m // 2].astype(jnp.float32), k)
            for j in range(4):
                part = upto[:width, 32 * j : 32 * j + 32]
                sums = upto[width + j : width + j + 1, :rows]
                state = jnp.where(same, jnp.concatenate([part] * 3, axis=1), 0.0)
                sums = jnp.where(same, jnp.broadcast_to(sums, (width, rows)), 0.0)
                left, left_low = split(jnp.concatenate([state, sums], axis=0))
                a, at = where[j, m]
                q, q_low = split(q_refs[a][at])
                both = dot(left, q, ((1,), (0,))) + dot(left_low, q, ((1,), (0,))) + dot(left, q_low, ((1,), (0,)))
                out_ref[j] = (both[:width] / (both[width:] + EPSILON)).astype(jnp.bfloat16)

    out = [jax.ShapeDtypeStruct((4, width, count), jnp.bfloat16)] * len(ms)
    ins = [VMEM] * (len(arrays) + 2 + len(planes))
    return call(body, out, ins, [], *arrays, mine, others, *[p for p, _, _ in planes])


def assemble(got):
    blocks, width, count = got[0].shape

    def body(*refs):
        *got_refs, out_ref, every = refs
        g, hi, b, _ = position()
        for m in range(4):
            this_g, this_b = jnp.bitwise_xor(g, m >> 1), jnp.bitwise_xor(b, m & 1)
            for k in range(blocks):
                at = ((jnp.bitwise_xor(hi, k) * 2 + this_b) * 2 + this_g) * width
                every[pl.ds(pl.multiple_of(at, 16), width)] = got_refs[m][k]
        out_ref[...] = every[...].T

    out = jax.ShapeDtypeStruct((count, 4 * blocks * width), jnp.bfloat16)
    scratch = [pltpu.VMEM((4 * blocks * width, count), jnp.bfloat16)]
    return call(body, out, [VMEM] * 4, scratch, *got)


def shared_plan(layout, frames_in, qkv_weight):
    weights = qkv_weight.transpose(0, 2, 1)
    width, depth = weights.shape[1:]
    half = HEAD_DIM // 2
    own = frames_in[0].T

    along = lambda k: layout.pairs(lambda g, hi, b, lo: (g, hi ^ k, b, lo))
    over_b = layout.pairs(lambda g, hi, b, lo: (g, hi, 1 - b, lo))
    over_g = layout.pairs(lambda g, hi, b, lo: (1 - g, hi, b, lo))
    over_gb = layout.pairs(lambda g, hi, b, lo: (1 - g, hi, 1 - b, lo))
    over_lo = layout.pairs(lambda g, hi, b, lo: (g, hi, b, 1 - lo))

    next_b = send(own, over_b)
    next_g = send(own, over_g)
    shard = weights.reshape(3 * width, depth)
    kv, q, whole, other_kv, other_q = pick(shard, send(shard, over_lo), half)
    more, kv_rows = q.shape[0], kv.shape[0]
    queries = {}

    def keep(made):
        places, array = made
        queries.update({km: (array, at) for km, at in places.items()})

    def swapped(a, first=0, rows=None):
        if rows is None:
            return [(a, send(a, over_lo), 0, 0, a.shape[0])]
        return [(a, send(a[first : first + rows], over_lo), first, 0, rows)]

    far_kv = send(kv, along(2))
    far_q = send(q, along(2))
    near = send(whole, along(1))
    next_b, next_g = lax.optimization_barrier((next_b, next_g))
    last_kv = send(far_kv, along(1))
    cut = depth // 2
    across = [send(next_b[:cut], over_g), send(next_g[cut:], over_b)]
    frames = [[own], [next_b], [next_g], across]
    blocks = [{"kv": [(kv, other_kv, 0, 0, kv_rows)], "q": [(q, other_q, 0, 0, more)]} for _ in range(4)]
    blocks[2]["kv"] = swapped(far_kv)
    blocks[1]["kv"] = swapped(near, 0, kv_rows)
    jobs = [([(k, "kv") for k in range(3)] + [(0, "q")], [0, 1, 2])]
    made, (_, states), given = project(half, jobs, blocks, frames, keep=True)
    keep(made)
    last_kv, states = lax.optimization_barrier((last_kv, states))
    blocks[3]["kv"] = swapped(last_kv)
    carried = [(m, states, m) for m in range(3)]
    ((_, states),) = project(half, [([(3, "kv")], [0, 1, 2])], blocks, frames, carried)
    *across, states = lax.optimization_barrier((*across, states))
    frames[3] = across
    ((_, states_3),) = project(half, [([(k, "kv") for k in range(3)], [3])], blocks, frames, given=given)
    last_q = send(far_q, along(1))
    blocks[2]["q"], blocks[3]["q"] = swapped(far_q), swapped(last_q)
    blocks[1]["q"] = swapped(near, kv_rows, more)
    carried = [(m, states, m) for m in range(3)] + [(3, states_3, 0)]
    ((_, mine),) = project(half, [([(3, "kv")], [3])], blocks, frames, carried)
    others = send(mine, over_lo)
    plane = plane_sum(mine, others)
    planes = [(send(plane, along(k)), k, lambda hi, k=k: jnp.bitwise_xor(hi, k) < hi) for k in (1, 2, 3)]
    last = [([(k, "q") for k in range(4)], [3]), ([(k, "q") for k in (1, 2, 3)], [0, 1, 2])]
    (made,) = project(half, last, blocks, frames)
    keep(made)

    out1, out2, out3 = apply(half, [1, 2, 3], queries, mine, others, planes)
    (out0,) = apply(half, [0], queries, mine, others, planes)
    out1 = send(out1, over_b)
    out2 = send(out2, over_g)
    out3 = send(out3, over_gb)
    return assemble([out0, out1, out2, out3])[None]


def solution(mesh):
    placed = (P(AXES, None, None), P(None, None, "frame"))

    def shards(frames_in, qkv_weight):
        width = qkv_weight.shape[2]
        if mesh.shape["groups"] == 2 and mesh.shape["frame"] == 16 and width * 2 == 5 * HEAD_DIM:
            return shared_plan(Layout(mesh), frames_in, qkv_weight)
        return gathered_plan(frames_in, qkv_weight)

    return jax.shard_map(
        shards, mesh=mesh, in_specs=placed, out_specs=P(AXES, None, None), check_vma=False
    )
```

```python
import jax
import jax.numpy as jnp
from jax import lax
from jax.experimental import pallas as pl
from jax.experimental.pallas import tpu as pltpu
from jax.sharding import PartitionSpec as P

HEAD_DIM = 32
EPSILON = 1e-06
AXES = ("groups", "frame")


def dot(a, b, dims):
    return lax.dot_general(a, b, (dims, ((), ())), preferred_element_type=jnp.float32)


def gathered_plan(frames_in, qkv_weight):
    tokens = frames_in[0]
    count = tokens.shape[0]
    weights = lax.all_gather(qkv_weight, "frame", axis=2, tiled=True)
    projected = jnp.einsum("td,sdc->stc", tokens, weights, preferred_element_type=jnp.float32)
    heads = weights.shape[2] // HEAD_DIM
    split = lambda a: a.reshape(count, heads, HEAD_DIM)
    queries = split(jax.nn.relu(projected[0]))
    keys = split(jax.nn.relu(projected[1].astype(jnp.bfloat16)))
    values = split(projected[2].astype(jnp.bfloat16))
    state = jnp.einsum("thi,thj->hij", keys, values, preferred_element_type=jnp.float32)
    key_sum = jnp.sum(keys.astype(jnp.float32), axis=0)
    both = jnp.concatenate([state, key_sum[:, :, None]], axis=2)
    everyone = lax.all_gather(both.reshape(heads, -1), "frame")
    upto = jnp.arange(everyone.shape[0]) <= lax.axis_index("frame")
    total = jnp.sum(jnp.where(upto[:, None, None], everyone, 0.0), axis=0).reshape(both.shape)
    result = jnp.einsum("thi,hij->thj", queries, total, precision=lax.Precision.HIGHEST)
    attended = result[..., :HEAD_DIM] / (result[..., HEAD_DIM:] + EPSILON)
    return attended.astype(jnp.bfloat16).reshape(1, count, -1)


class Layout:
    def __init__(self, mesh):
        self.frames = mesh.shape["frame"]
        self.lows = 2
        self.highs = self.frames // 4

    def pairs(self, target, source=lambda g, hi, b, lo: True):
        out = []
        for g in range(2):
            for hi in range(self.highs):
                for b in range(2):
                    for lo in range(self.lows):
                        if source(g, hi, b, lo):
                            to = target(g, hi, b, lo)
                            out.append((self.place(g, hi, b, lo), self.place(*to)))
        return out

    def place(self, g, hi, b, lo):
        return ((g * self.highs + hi) * 2 + b) * self.lows + lo


def send(a, pairs):
    return lax.ppermute(a, AXES, pairs)


ANY = pl.BlockSpec(memory_space=pl.ANY)
VMEM = pl.BlockSpec(memory_space=pltpu.VMEM)
LIGHT = pl.CostEstimate(flops=1000, bytes_accessed=1000, transcendentals=0)


def position():
    frame = lax.axis_index("frame")
    return lax.axis_index("groups"), frame // 4, (frame // 2) % 2, frame % 2


def call(body, out, ins, scratch, *operands):
    return pl.pallas_call(
        body,
        out_shape=out,
        in_specs=ins,
        out_specs=jax.tree.map(lambda _: VMEM, out),
        scratch_shapes=scratch,
        compiler_params=pltpu.CompilerParams(vmem_limit_bytes=16 * 2**20),
        cost_estimate=LIGHT,
    )(*operands)


def heads_of(g, width, half):
    shape = (width, width + half)
    row = lax.broadcasted_iota(jnp.int32, shape, 0)
    column = lax.broadcasted_iota(jnp.int32, shape, 1)
    turned = column + half * g
    turned = jnp.where(turned >= width + half, turned - (width + half), turned)
    return (width * g + row) // HEAD_DIM == (4 * half * g + turned) // HEAD_DIM


def pick(own, swapped, half):
    width, depth = own.shape[0] // 3, own.shape[1]
    part = -(-depth // 256) * 128
    more = width + half
    rows = 2 * more + width

    def body(own_ref, swapped_ref, kv_ref, q_ref, all_ref, other_kv_ref, other_q_ref, full):
        g, _, _, lo = position()
        mine = lo == g
        full[:, 2 * part - 128 :] = jnp.zeros((rows, 128), full.dtype)
        at = pl.multiple_of(g * (width - half), 16)
        for start, which in ((0, 1), (more, 2), (more + width, 0)):
            shard = pl.ds(which * width, width)
            full[start : start + width, :depth] = jnp.where(mine, own_ref[shard], swapped_ref[shard])
            if which < 2:
                extra = pl.ds(which * width + at, half)
                full[start + width : start + more, :depth] = jnp.where(mine, swapped_ref[extra], own_ref[extra])
        this = full[:, pl.ds(pl.multiple_of(lo * part, 128), part)]
        that = full[:, pl.ds(pl.multiple_of((1 - lo) * part, 128), part)]
        kv_ref[...] = this[: more + width]
        q_ref[...] = this[more + width :]
        all_ref[...] = this
        other_kv_ref[...] = that[: more + width]
        other_q_ref[...] = that[more + width :]

    shape = lambda n: jax.ShapeDtypeStruct((n, part), own.dtype)
    out = [shape(more + width), shape(more), shape(rows), shape(more + width), shape(more)]
    return call(body, out, [VMEM, VMEM], [pltpu.VMEM((rows, 2 * part), own.dtype)], own, swapped)


def project(half, jobs, blocks, frames, carried=(), keep=False, given=None):
    arrays, pieces, rows = [], {}, 0

    def index(a):
        for i, b in enumerate(arrays):
            if a is b:
                return i
        arrays.append(a)
        return len(arrays) - 1

    more = 3 * HEAD_DIM
    width = more - half
    tall = {"kv": more + width, "q": more}
    for named, ms in jobs:
        for k, what in named:
            if (k, what) not in pieces:
                chunks = [(index(one), index(two), *at) for one, two, *at in blocks[k][what]]
                pieces[k, what] = (chunks, rows)
                rows += tall[what]
    if given is not None:
        pieces, rows = given[0], 0
    parts = {m: [index(p) for p in frames[m]] for _, ms in jobs for m in ms}
    count = frames[0][0].shape[1]
    depth = frames[0][0].shape[0]
    part = arrays[0].shape[1]
    if given is not None:
        arrays = [given[1]]
        parts = {m: [index(p) for p in frames[m]] for _, ms in jobs for m in ms}
    held = sorted({m for named, ms in jobs for m in ms if any(w == "kv" for _, w in named)} | {m for m, _, _ in carried})
    places = {}
    for named, ms in jobs:
        for m in ms:
            for k, what in named:
                if what == "q":
                    places[k, m] = len(places)
    n_in = len(arrays)

    def body(*refs):
        ins, refs = refs[:n_in], list(refs[n_in:])
        c_refs = [refs.pop(0) for _ in carried]
        q_ref = refs.pop(0) if places else None
        s_ref = refs.pop(0) if held else None
        w_ref = refs.pop(0) if given is None else ins[0]
        g, _, _, lo = position()
        first_half = lo == 0
        if held:
            same = heads_of(g, width, half)
            ones = jnp.ones((8, count), jnp.bfloat16)
            s_ref[...] = jnp.zeros_like(s_ref)
            for (m, _, at), c_ref in zip(carried, c_refs):
                s_ref[held.index(m)] = c_ref[at]
        for chunks, at in [] if given is not None else pieces.values():
            for one, two, first, second, n in chunks:
                one, two = ins[one][first : first + n], ins[two][second : second + n]
                w_ref[at : at + n, :part] = jnp.where(first_half, one, two)
                w_ref[at : at + n, part:] = jnp.where(first_half, two, one)[:, : depth - part]
                at += n
        for named, ms in jobs:
            start = pieces[named[0]][1]
            stop = pieces[named[-1]][1] + tall[named[-1][1]]
            for m in ms:
                x = [ins[p][...] for p in parts[m]]
                x = jnp.concatenate(x, axis=0) if len(x) > 1 else x[0]
                all_made = dot(w_ref[start:stop], x, ((1,), (0,)))
                for k, what in named:
                    at = pieces[k, what][1] - start
                    made = all_made[at : at + tall[what]]
                    if what == "q":
                        q_ref[places[k, m]] = jnp.maximum(made, 0.0)
                        continue
                    keys = jnp.maximum(made[:more], 0.0).astype(jnp.bfloat16)
                    values = made[more:].astype(jnp.bfloat16)
                    full = jnp.where(same, dot(values, keys, ((1,), (1,))), 0.0)
                    at = held.index(m)
                    s_ref[at, :width, 32 * k : 32 * k + 32] = full[:, :32] + full[:, 32:64] + full[:, 64:]
                    s_ref[at, width + k : width + k + 1, :more] = dot(ones, keys, ((1,), (1,)))[:1]

    out = []
    if places:
        out.append(jax.ShapeDtypeStruct((len(places), more, count), jnp.float32))
    if held:
        out.append(jax.ShapeDtypeStruct((len(held), width + 16, 128), jnp.float32))
    scratch = []
    if keep:
        out.append(jax.ShapeDtypeStruct((rows, depth), jnp.bfloat16))
    elif given is None:
        scratch.append(pltpu.VMEM((rows, depth), jnp.bfloat16))
    ins = [VMEM] * (n_in + len(carried))
    got = list(call(body, out, ins, scratch, *arrays, *[a for _, a, _ in carried]))
    made = ([(places, got.pop(0))] if places else []) + ([(held, got.pop(0))] if held else [])
    return made + ([(pieces, got[0])] if keep else [])


def plane_sum(mine, others):
    def body(a_ref, b_ref, out_ref):
        both = a_ref[...] + b_ref[...]
        out_ref[0] = (both[0] + both[1]).astype(out_ref.dtype)
        out_ref[1] = (both[2] + both[3]).astype(out_ref.dtype)

    out = jax.ShapeDtypeStruct((2,) + mine.shape[1:], jnp.bfloat16)
    return call(body, out, [VMEM] * 2, [], mine, others)


def turn(a, k):
    lanes = [a[..., 32 * (j ^ k) : 32 * (j ^ k) + 32] for j in range(4)]
    rows = a.shape[-2] - 16
    sums = [a[..., rows + (j ^ k) : rows + (j ^ k) + 1, :] for j in range(4)]
    return jnp.concatenate([jnp.concatenate(lanes, axis=-1)[..., :rows, :], *sums, a[..., rows + 4 :, :]], axis=-2)


def apply(half, ms, queries, mine, others, planes):
    arrays = []
    where = {}
    for m in ms:
        for k in range(4):
            a, at = queries[k, m]
            if not any(a is b for b in arrays):
                arrays.append(a)
            where[k, m] = ([a is b for b in arrays].index(True), at)
    rows, count = arrays[0].shape[1:]
    width = rows - half

    def body(*refs):
        q_refs = refs[: len(arrays)]
        mine_ref, others_ref = refs[len(arrays) : len(arrays) + 2]
        plane_refs, outs = refs[len(arrays) + 2 : -len(ms)], refs[-len(ms) :]
        g, hi, b, lo = position()
        same = heads_of(g, width, half)
        factor = lambda yes: jnp.where(yes, 1.0, 0.0).astype(jnp.float32)
        second = factor(lo == 1)

        def split(a):
            high = a.astype(jnp.bfloat16)
            return high, (a - high.astype(jnp.float32)).astype(jnp.bfloat16)

        for out_ref, m in zip(outs, ms):
            after = factor(jnp.bitwise_xor(b, m & 1) == 1)
            upto = mine_ref[m] + second * others_ref[m] + after * (mine_ref[m ^ 1] + others_ref[m ^ 1])
            for ref, (_, k, adds) in zip(plane_refs, planes):
                upto += factor(adds(hi)) * turn(ref[m // 2].astype(jnp.float32), k)
            for j in range(4):
                part = upto[:width, 32 * j : 32 * j + 32]
                sums = upto[width + j : width + j + 1, :rows]
                state = jnp.where(same, jnp.concatenate([part] * 3, axis=1), 0.0)
                sums = jnp.where(same, jnp.broadcast_to(sums, (width, rows)), 0.0)
                left, left_low = split(jnp.concatenate([state, sums], axis=0))
                a, at = where[j, m]
                q, q_low = split(q_refs[a][at])
                both = dot(left, q, ((1,), (0,))) + dot(left_low, q, ((1,), (0,))) + dot(left, q_low, ((1,), (0,)))
                out_ref[j] = (both[:width] / (both[width:] + EPSILON)).astype(jnp.bfloat16)

    out = [jax.ShapeDtypeStruct((4, width, count), jnp.bfloat16)] * len(ms)
    ins = [VMEM] * (len(arrays) + 2 + len(planes))
    return call(body, out, ins, [], *arrays, mine, others, *[p for p, _, _ in planes])


def assemble(got):
    blocks, width, count = got[0].shape

    def body(*refs):
        *got_refs, out_ref, every = refs
        g, hi, b, _ = position()
        for m in range(4):
            this_g, this_b = jnp.bitwise_xor(g, m >> 1), jnp.bitwise_xor(b, m & 1)
            for k in range(blocks):
                at = ((jnp.bitwise_xor(hi, k) * 2 + this_b) * 2 + this_g) * width
                every[pl.ds(pl.multiple_of(at, 16), width)] = got_refs[m][k]
        out_ref[...] = every[...].T

    out = jax.ShapeDtypeStruct((count, 4 * blocks * width), jnp.bfloat16)
    scratch = [pltpu.VMEM((4 * blocks * width, count), jnp.bfloat16)]
    return call(body, out, [VMEM] * 4, scratch, *got)


def shared_plan(layout, frames_in, qkv_weight):
    weights = qkv_weight.transpose(0, 2, 1)
    width, depth = weights.shape[1:]
    half = HEAD_DIM // 2
    own = frames_in[0].T

    along = lambda k: layout.pairs(lambda g, hi, b, lo: (g, hi ^ k, b, lo))
    over_b = layout.pairs(lambda g, hi, b, lo: (g, hi, 1 - b, lo))
    over_g = layout.pairs(lambda g, hi, b, lo: (1 - g, hi, b, lo))
    over_gb = layout.pairs(lambda g, hi, b, lo: (1 - g, hi, 1 - b, lo))
    over_lo = layout.pairs(lambda g, hi, b, lo: (g, hi, b, 1 - lo))

    next_b = send(own, over_b)
    next_g = send(own, over_g)
    shard = weights.reshape(3 * width, depth)
    kv, q, whole, other_kv, other_q = pick(shard, send(shard, over_lo), half)
    more, kv_rows = q.shape[0], kv.shape[0]
    queries = {}

    def keep(made):
        places, array = made
        queries.update({km: (array, at) for km, at in places.items()})

    def swapped(a, first=0, rows=None):
        if rows is None:
            return [(a, send(a, over_lo), 0, 0, a.shape[0])]
        return [(a, send(a[first : first + rows], over_lo), first, 0, rows)]

    far_kv = send(kv, along(2))
    far_q = send(q, along(2))
    near = send(whole, along(1))
    next_b, next_g = lax.optimization_barrier((next_b, next_g))
    last_kv = send(far_kv, along(1))
    cut = depth // 2
    across = [send(next_b[:cut], over_g), send(next_g[cut:], over_b)]
    frames = [[own], [next_b], [next_g], across]
    blocks = [{"kv": [(kv, other_kv, 0, 0, kv_rows)], "q": [(q, other_q, 0, 0, more)]} for _ in range(4)]
    blocks[2]["kv"] = swapped(far_kv)
    blocks[1]["kv"] = swapped(near, 0, kv_rows)
    jobs = [([(k, "kv") for k in range(3)] + [(0, "q")], [0, 1, 2])]
    made, (_, states), given = project(half, jobs, blocks, frames, keep=True)
    keep(made)
    last_kv, states = lax.optimization_barrier((last_kv, states))
    blocks[3]["kv"] = swapped(last_kv)
    carried = [(m, states, m) for m in range(3)]
    ((_, states),) = project(half, [([(3, "kv")], [0, 1, 2])], blocks, frames, carried)
    *across, states = lax.optimization_barrier((*across, states))
    frames[3] = across
    ((_, states_3),) = project(half, [([(k, "kv") for k in range(3)], [3])], blocks, frames, given=given)
    last_q = send(far_q, along(1))
    blocks[2]["q"], blocks[3]["q"] = swapped(far_q), swapped(last_q)
    blocks[1]["q"] = swapped(near, kv_rows, more)
    carried = [(m, states, m) for m in range(3)] + [(3, states_3, 0)]
    ((_, mine),) = project(half, [([(3, "kv")], [3])], blocks, frames, carried)
    others = send(mine, over_lo)
    plane = plane_sum(mine, others)
    planes = [(send(plane, along(k)), k, lambda hi, k=k: jnp.bitwise_xor(hi, k) < hi) for k in (3, 2, 1)]
    last = [([(k, "q") for k in range(4)], [3]), ([(k, "q") for k in (1, 2, 3)], [0, 1, 2])]
    (made,) = project(half, last, blocks, frames)
    keep(made)

    (out3,) = apply(half, [3], queries, mine, others, planes)
    out2, out1 = apply(half, [2, 1], queries, mine, others, planes)
    (out0,) = apply(half, [0], queries, mine, others, planes)
    out1 = send(out1, over_b)
    out2 = send(out2, over_g)
    out3 = send(out3, over_gb)
    return assemble([out0, out1, out2, out3])[None]


def solution(mesh):
    placed = (P(AXES, None, None), P(None, None, "frame"))

    def shards(frames_in, qkv_weight):
        width = qkv_weight.shape[2]
        if mesh.shape["groups"] == 2 and mesh.shape["frame"] == 16 and width * 2 == 5 * HEAD_DIM:
            return shared_plan(Layout(mesh), frames_in, qkv_weight)
        return gathered_plan(frames_in, qkv_weight)

    return jax.shard_map(
        shards, mesh=mesh, in_specs=placed, out_specs=P(AXES, None, None), check_vma=False
    )
```

```python
import jax
import jax.numpy as jnp
from jax import lax
from jax.experimental import pallas as pl
from jax.experimental.pallas import tpu as pltpu
from jax.sharding import PartitionSpec as P

HEAD_DIM = 32
EPSILON = 1e-06
AXES = ("groups", "frame")


def dot(a, b, dims):
    return lax.dot_general(a, b, (dims, ((), ())), preferred_element_type=jnp.float32)


def gathered_plan(frames_in, qkv_weight):
    tokens = frames_in[0]
    count = tokens.shape[0]
    weights = lax.all_gather(qkv_weight, "frame", axis=2, tiled=True)
    projected = jnp.einsum("td,sdc->stc", tokens, weights, preferred_element_type=jnp.float32)
    heads = weights.shape[2] // HEAD_DIM
    split = lambda a: a.reshape(count, heads, HEAD_DIM)
    queries = split(jax.nn.relu(projected[0]))
    keys = split(jax.nn.relu(projected[1].astype(jnp.bfloat16)))
    values = split(projected[2].astype(jnp.bfloat16))
    state = jnp.einsum("thi,thj->hij", keys, values, preferred_element_type=jnp.float32)
    key_sum = jnp.sum(keys.astype(jnp.float32), axis=0)
    both = jnp.concatenate([state, key_sum[:, :, None]], axis=2)
    everyone = lax.all_gather(both.reshape(heads, -1), "frame")
    upto = jnp.arange(everyone.shape[0]) <= lax.axis_index("frame")
    total = jnp.sum(jnp.where(upto[:, None, None], everyone, 0.0), axis=0).reshape(both.shape)
    result = jnp.einsum("thi,hij->thj", queries, total, precision=lax.Precision.HIGHEST)
    attended = result[..., :HEAD_DIM] / (result[..., HEAD_DIM:] + EPSILON)
    return attended.astype(jnp.bfloat16).reshape(1, count, -1)


class Layout:
    def __init__(self, mesh):
        self.frames = mesh.shape["frame"]
        self.lows = 2
        self.highs = self.frames // 4

    def pairs(self, target, source=lambda g, hi, b, lo: True):
        out = []
        for g in range(2):
            for hi in range(self.highs):
                for b in range(2):
                    for lo in range(self.lows):
                        if source(g, hi, b, lo):
                            to = target(g, hi, b, lo)
                            out.append((self.place(g, hi, b, lo), self.place(*to)))
        return out

    def place(self, g, hi, b, lo):
        return ((g * self.highs + hi) * 2 + b) * self.lows + lo


def send(a, pairs):
    return lax.ppermute(a, AXES, pairs)


ANY = pl.BlockSpec(memory_space=pl.ANY)
VMEM = pl.BlockSpec(memory_space=pltpu.VMEM)
LIGHT = pl.CostEstimate(flops=1000, bytes_accessed=1000, transcendentals=0)


def position():
    frame = lax.axis_index("frame")
    return lax.axis_index("groups"), frame // 4, (frame // 2) % 2, frame % 2


def call(body, out, ins, scratch, *operands):
    return pl.pallas_call(
        body,
        out_shape=out,
        in_specs=ins,
        out_specs=jax.tree.map(lambda _: VMEM, out),
        scratch_shapes=scratch,
        compiler_params=pltpu.CompilerParams(vmem_limit_bytes=8 * 2**20),
        cost_estimate=LIGHT,
    )(*operands)


def heads_of(g, width, half):
    shape = (width, width + half)
    row = lax.broadcasted_iota(jnp.int32, shape, 0)
    column = lax.broadcasted_iota(jnp.int32, shape, 1)
    turned = column + half * g
    turned = jnp.where(turned >= width + half, turned - (width + half), turned)
    return (width * g + row) // HEAD_DIM == (4 * half * g + turned) // HEAD_DIM


def pick(own, swapped, half):
    width, depth = own.shape[0] // 3, own.shape[1]
    part = -(-depth // 256) * 128
    more = width + half
    rows = 2 * more + width

    def body(own_ref, swapped_ref, kv_ref, q_ref, all_ref, other_kv_ref, other_q_ref, full):
        g, _, _, lo = position()
        mine = lo == g
        full[:, 2 * part - 128 :] = jnp.zeros((rows, 128), full.dtype)
        at = pl.multiple_of(g * (width - half), 16)
        for start, which in ((0, 1), (more, 2), (more + width, 0)):
            shard = pl.ds(which * width, width)
            full[start : start + width, :depth] = jnp.where(mine, own_ref[shard], swapped_ref[shard])
            if which < 2:
                extra = pl.ds(which * width + at, half)
                full[start + width : start + more, :depth] = jnp.where(mine, swapped_ref[extra], own_ref[extra])
        this = full[:, pl.ds(pl.multiple_of(lo * part, 128), part)]
        that = full[:, pl.ds(pl.multiple_of((1 - lo) * part, 128), part)]
        kv_ref[...] = this[: more + width]
        q_ref[...] = this[more + width :]
        all_ref[...] = this
        other_kv_ref[...] = that[: more + width]
        other_q_ref[...] = that[more + width :]

    shape = lambda n: jax.ShapeDtypeStruct((n, part), own.dtype)
    out = [shape(more + width), shape(more), shape(rows), shape(more + width), shape(more)]
    return call(body, out, [VMEM, VMEM], [pltpu.VMEM((rows, 2 * part), own.dtype)], own, swapped)


def project(half, jobs, blocks, frames, carried=(), keep=False, given=None):
    arrays, pieces, rows = [], {}, 0

    def index(a):
        for i, b in enumerate(arrays):
            if a is b:
                return i
        arrays.append(a)
        return len(arrays) - 1

    more = 3 * HEAD_DIM
    width = more - half
    tall = {"kv": more + width, "q": more}
    for named, ms in jobs:
        for k, what in named:
            if (k, what) not in pieces:
                chunks = [(index(one), index(two), *at) for one, two, *at in blocks[k][what]]
                pieces[k, what] = (chunks, rows)
                rows += tall[what]
    if given is not None:
        pieces, rows = given[0], 0
    parts = {m: [index(p) for p in frames[m]] for _, ms in jobs for m in ms}
    count = frames[0][0].shape[1]
    depth = frames[0][0].shape[0]
    part = arrays[0].shape[1]
    if given is not None:
        arrays = [given[1]]
        parts = {m: [index(p) for p in frames[m]] for _, ms in jobs for m in ms}
    held = sorted({m for named, ms in jobs for m in ms if any(w == "kv" for _, w in named)} | {m for m, _, _ in carried})
    places = {}
    for named, ms in jobs:
        for m in ms:
            for k, what in named:
                if what == "q":
                    places[k, m] = len(places)
    n_in = len(arrays)

    def body(*refs):
        ins, refs = refs[:n_in], list(refs[n_in:])
        c_refs = [refs.pop(0) for _ in carried]
        q_ref = refs.pop(0) if places else None
        s_ref = refs.pop(0) if held else None
        w_ref = refs.pop(0) if given is None else ins[0]
        g, _, _, lo = position()
        first_half = lo == 0
        if held:
            same = heads_of(g, width, half)
            ones = jnp.ones((8, count), jnp.bfloat16)
            s_ref[...] = jnp.zeros_like(s_ref)
            for (m, _, at), c_ref in zip(carried, c_refs):
                s_ref[held.index(m)] = c_ref[at]
        for chunks, at in [] if given is not None else pieces.values():
            for one, two, first, second, n in chunks:
                one, two = ins[one][first : first + n], ins[two][second : second + n]
                w_ref[at : at + n, :part] = jnp.where(first_half, one, two)
                w_ref[at : at + n, part:] = jnp.where(first_half, two, one)[:, : depth - part]
                at += n
        for named, ms in jobs:
            start = pieces[named[0]][1]
            stop = pieces[named[-1]][1] + tall[named[-1][1]]
            for m in ms:
                all_made, at = 0.0, 0
                for p in parts[m]:
                    n = ins[p].shape[0]
                    all_made += dot(w_ref[start:stop, at : at + n], ins[p][...], ((1,), (0,)))
                    at += n
                for k, what in named:
                    at = pieces[k, what][1] - start
                    made = all_made[at : at + tall[what]]
                    if what == "q":
                        q_ref[places[k, m]] = jnp.maximum(made, 0.0)
                        continue
                    keys = jnp.maximum(made[:more], 0.0).astype(jnp.bfloat16)
                    values = made[more:].astype(jnp.bfloat16)
                    full = jnp.where(same, dot(values, keys, ((1,), (1,))), 0.0)
                    at = held.index(m)
                    s_ref[at, :width, 32 * k : 32 * k + 32] = full[:, :32] + full[:, 32:64] + full[:, 64:]
                    s_ref[at, width + k : width + k + 1, :more] = dot(ones, keys, ((1,), (1,)))[:1]

    out = []
    if places:
        out.append(jax.ShapeDtypeStruct((len(places), more, count), jnp.float32))
    if held:
        out.append(jax.ShapeDtypeStruct((len(held), width + 16, 128), jnp.float32))
    scratch = []
    if keep:
        out.append(jax.ShapeDtypeStruct((rows, depth), jnp.bfloat16))
    elif given is None:
        scratch.append(pltpu.VMEM((rows, depth), jnp.bfloat16))
    ins = [VMEM] * (n_in + len(carried))
    got = list(call(body, out, ins, scratch, *arrays, *[a for _, a, _ in carried]))
    made = ([(places, got.pop(0))] if places else []) + ([(held, got.pop(0))] if held else [])
    return made + ([(pieces, got[0])] if keep else [])


def plane_sum(mine, others):
    def body(a_ref, b_ref, out_ref):
        both = a_ref[...] + b_ref[...]
        out_ref[0] = (both[0] + both[1]).astype(out_ref.dtype)
        out_ref[1] = (both[2] + both[3]).astype(out_ref.dtype)

    out = jax.ShapeDtypeStruct((2,) + mine.shape[1:], jnp.bfloat16)
    return call(body, out, [VMEM] * 2, [], mine, others)


def turn(a, k):
    lanes = [a[..., 32 * (j ^ k) : 32 * (j ^ k) + 32] for j in range(4)]
    rows = a.shape[-2] - 16
    sums = [a[..., rows + (j ^ k) : rows + (j ^ k) + 1, :] for j in range(4)]
    return jnp.concatenate([jnp.concatenate(lanes, axis=-1)[..., :rows, :], *sums, a[..., rows + 4 :, :]], axis=-2)


def apply(half, ms, queries, mine, others, planes):
    arrays = []
    where = {}
    for m in ms:
        for k in range(4):
            a, at = queries[k, m]
            if not any(a is b for b in arrays):
                arrays.append(a)
            where[k, m] = ([a is b for b in arrays].index(True), at)
    rows, count = arrays[0].shape[1:]
    width = rows - half

    def body(*refs):
        q_refs = refs[: len(arrays)]
        mine_ref, others_ref = refs[len(arrays) : len(arrays) + 2]
        plane_refs, outs = refs[len(arrays) + 2 : -len(ms)], refs[-len(ms) :]
        g, hi, b, lo = position()
        same = heads_of(g, width, half)
        factor = lambda yes: jnp.where(yes, 1.0, 0.0).astype(jnp.float32)
        second = factor(lo == 1)

        def split(a):
            high = a.astype(jnp.bfloat16)
            return high, (a - high.astype(jnp.float32)).astype(jnp.bfloat16)

        for out_ref, m in zip(outs, ms):
            after = factor(jnp.bitwise_xor(b, m & 1) == 1)
            upto = mine_ref[m] + second * others_ref[m] + after * (mine_ref[m ^ 1] + others_ref[m ^ 1])
            for ref, (_, k, adds) in zip(plane_refs, planes):
                upto += factor(adds(hi)) * turn(ref[m // 2].astype(jnp.float32), k)
            for j in range(4):
                part = upto[:width, 32 * j : 32 * j + 32]
                sums = upto[width + j : width + j + 1, :rows]
                state = jnp.where(same, jnp.concatenate([part] * 3, axis=1), 0.0)
                sums = jnp.where(same, jnp.broadcast_to(sums, (width, rows)), 0.0)
                left, left_low = split(jnp.concatenate([state, sums], axis=0))
                a, at = where[j, m]
                q, q_low = split(q_refs[a][at])
                both = dot(left, q, ((1,), (0,))) + dot(left_low, q, ((1,), (0,))) + dot(left, q_low, ((1,), (0,)))
                out_ref[j] = (both[:width] / (both[width:] + EPSILON)).astype(jnp.bfloat16)

    out = [jax.ShapeDtypeStruct((4, width, count), jnp.bfloat16)] * len(ms)
    ins = [VMEM] * (len(arrays) + 2 + len(planes))
    return call(body, out, ins, [], *arrays, mine, others, *[p for p, _, _ in planes])


def assemble(got):
    blocks, width, count = got[0].shape

    def body(*refs):
        *got_refs, out_ref, every = refs
        g, hi, b, _ = position()
        for m in range(4):
            this_g, this_b = jnp.bitwise_xor(g, m >> 1), jnp.bitwise_xor(b, m & 1)
            for k in range(blocks):
                at = ((jnp.bitwise_xor(hi, k) * 2 + this_b) * 2 + this_g) * width
                every[pl.ds(pl.multiple_of(at, 16), width)] = got_refs[m][k]
        out_ref[...] = every[...].T

    out = jax.ShapeDtypeStruct((count, 4 * blocks * width), jnp.bfloat16)
    scratch = [pltpu.VMEM((4 * blocks * width, count), jnp.bfloat16)]
    return call(body, out, [VMEM] * 4, scratch, *got)


def shared_plan(layout, frames_in, qkv_weight):
    weights = qkv_weight.transpose(0, 2, 1)
    width, depth = weights.shape[1:]
    half = HEAD_DIM // 2
    own = frames_in[0].T

    along = lambda k: layout.pairs(lambda g, hi, b, lo: (g, hi ^ k, b, lo))
    over_b = layout.pairs(lambda g, hi, b, lo: (g, hi, 1 - b, lo))
    over_g = layout.pairs(lambda g, hi, b, lo: (1 - g, hi, b, lo))
    over_gb = layout.pairs(lambda g, hi, b, lo: (1 - g, hi, 1 - b, lo))
    over_lo = layout.pairs(lambda g, hi, b, lo: (g, hi, b, 1 - lo))

    next_b = send(own, over_b)
    next_g = send(own, over_g)
    shard = weights.reshape(3 * width, depth)
    kv, q, whole, other_kv, other_q = pick(shard, send(shard, over_lo), half)
    more, kv_rows = q.shape[0], kv.shape[0]
    queries = {}

    def keep(made):
        places, array = made
        queries.update({km: (array, at) for km, at in places.items()})

    def swapped(a, first=0, rows=None):
        if rows is None:
            return [(a, send(a, over_lo), 0, 0, a.shape[0])]
        return [(a, send(a[first : first + rows], over_lo), first, 0, rows)]

    far_kv = send(kv, along(2))
    far_q = send(q, along(2))
    near = send(whole, along(1))
    next_b, next_g = lax.optimization_barrier((next_b, next_g))
    last_kv = send(far_kv, along(1))
    cut = depth // 512 * 256
    across = [send(next_b[:cut], over_g), send(next_g[cut:], over_b)]
    frames = [[own], [next_b], [next_g], across]
    blocks = [{"kv": [(kv, other_kv, 0, 0, kv_rows)], "q": [(q, other_q, 0, 0, more)]} for _ in range(4)]
    blocks[2]["kv"] = swapped(far_kv)
    blocks[1]["kv"] = swapped(near, 0, kv_rows)
    jobs = [([(k, "kv") for k in range(3)] + [(0, "q")], [0, 1, 2])]
    made, (_, states), given = project(half, jobs, blocks, frames, keep=True)
    keep(made)
    last_kv, states = lax.optimization_barrier((last_kv, states))
    blocks[3]["kv"] = swapped(last_kv)
    carried = [(m, states, m) for m in range(3)]
    ((_, states),) = project(half, [([(3, "kv")], [0, 1, 2])], blocks, frames, carried)
    *across, states = lax.optimization_barrier((*across, states))
    frames[3] = across
    ((_, states_3),) = project(half, [([(k, "kv") for k in range(3)], [3])], blocks, frames, given=given)
    last_q = send(far_q, along(1))
    blocks[2]["q"], blocks[3]["q"] = swapped(far_q), swapped(last_q)
    blocks[1]["q"] = swapped(near, kv_rows, more)
    carried = [(m, states, m) for m in range(3)] + [(3, states_3, 0)]
    ((_, mine),) = project(half, [([(3, "kv")], [3])], blocks, frames, carried)
    others = send(mine, over_lo)
    plane = plane_sum(mine, others)
    planes = [(send(plane, along(k)), k, lambda hi, k=k: jnp.bitwise_xor(hi, k) < hi) for k in (3, 2, 1)]
    last = [([(k, "q") for k in range(4)], [3]), ([(k, "q") for k in (1, 2, 3)], [0, 1, 2])]
    (made,) = project(half, last, blocks, frames)
    keep(made)

    (out3,) = apply(half, [3], queries, mine, others, planes)
    out2, out1 = apply(half, [2, 1], queries, mine, others, planes)
    (out0,) = apply(half, [0], queries, mine, others, planes)
    out1 = send(out1, over_b)
    out2 = send(out2, over_g)
    out3 = send(out3, over_gb)
    return assemble([out0, out1, out2, out3])[None]


def solution(mesh):
    placed = (P(AXES, None, None), P(None, None, "frame"))

    def shards(frames_in, qkv_weight):
        width = qkv_weight.shape[2]
        if mesh.shape["groups"] == 2 and mesh.shape["frame"] == 16 and width * 2 == 5 * HEAD_DIM:
            return shared_plan(Layout(mesh), frames_in, qkv_weight)
        return gathered_plan(frames_in, qkv_weight)

    return jax.shard_map(
        shards, mesh=mesh, in_specs=placed, out_specs=P(AXES, None, None), check_vma=False
    )
```
